512 devices in a mesh: dp: 64 (over x, z, core), tensor: 8 (over y).
Axes of the slice: x: 4, y: 8, z: 8, core: 2. Of those that a mesh axis runs over, the one named last changes fastest.
Arguments:
- prompt_keys: bfloat16 [4096, 1024], P('dp', 'tensor'), may hold values from -6 to 6
- prompt_values: bfloat16 [4096, 1024], P('dp', 'tensor'), may hold values from -6 to 6
- key_weight: bfloat16 [5120, 1024], P('dp', 'tensor'), may hold values from -0.078125 to 0.078125
- value_weight: bfloat16 [5120, 1024], P('dp', 'tensor'), may hold values from -0.078125 to 0.078125
- resp_query: bfloat16 [8192, 8192], P('dp', 'tensor'), may hold values from -6 to 6
- resp_keys: bfloat16 [8192, 1024], P('dp', 'tensor'), may hold values from -6 to 6
- resp_values: bfloat16 [8192, 1024], P('dp', 'tensor'), may hold values from -6 to 6
- resp_grad: bfloat16 [8192, 8192], P('dp', 'tensor'), may hold values from -48 to 48
- resp_lse: float32 [64, 8192], P('tensor', 'dp'), as said below
- resp_delta: float32 [64, 8192], P('tensor', 'dp'), may hold values from -24 to 24
- resp_prompt: int32 [1024], replicated, may hold values from 0 to 63, as said below
- resp_lengths: int32 [1024], P('dp'), may hold values from 1 to 8, 5120 in all
Outputs:
- d_query: bfloat16 [8192, 8192], P('dp', 'tensor')
- d_resp_keys: bfloat16 [8192, 1024], P('dp', 'tensor')
- d_resp_values: bfloat16 [8192, 1024], P('dp', 'tensor')
- d_prompt_input: bfloat16 [4096, 5120], P('dp', 'tensor')
The draws below stay inside these ranges and needn't reach their ends.
Inputs may be any that keep to these rules, and one draw needn't show every extreme that they name: `resp_prompt`: response r sits on index r // 16 of dp, in slot r % 16, and prompt p on index p. For each slot number s, the responses in slot s of all indices of dp name every prompt exactly once; so each prompt is named by exactly 16 responses, and the 16 responses of one index of dp name 16 different prompts. `resp_lse`: within 0.5 below and 1.5 above log(72).
All inputs are finite; a program needn't handle non-finite values. No bound on the sum of `resp_lengths` on one device may be relied on, other than what follows from the above.
Results may differ from the reference program's by a relative error of at most 0.006.
Values may be sent and summed in bfloat16 or wider, within the bound.
A program may use at most 64 MiB of HBM per device.

```python
import math
import jax
import jax.numpy as jnp
import numpy as np
from jax import lax

D = 5120
QH = 64
KVH = 8
HD = 128
GROUP = 16
LP = 64
LR = 8
PROMPTS = 64
RESPONSES = 1024


def draw_resp_prompt(key, part):
    key = jax.random.fold_in(key, 11)
    first_key, second_key = jax.random.split(key)
    offsets = jax.random.permutation(first_key, PROMPTS)[:GROUP]
    relabel = jax.random.permutation(second_key, PROMPTS)
    device_ids = jnp.arange(PROMPTS)[:, None]
    placed = relabel[(device_ids + offsets[None, :]) % PROMPTS]
    return placed.reshape(-1).astype(jnp.int32)


def draw_resp_lse(key, part):
    key = jax.random.fold_in(key, 23)
    spread = jax.random.uniform(key, (QH, RESPONSES * LR), jnp.float32, 0.0, 1.0)
    return jnp.log(jnp.float32(LP + LR)) + spread


def block_levels(key, shape, shards, low, top_value):
    def one(dim, blocks):
        draws = jax.random.uniform(jax.random.fold_in(jax.random.fold_in(key, 6), dim), (blocks,), jnp.float32, low / len(shards), top_value / len(shards))
        return jnp.repeat(jnp.exp(draws), shape[dim] // blocks).reshape((-1,) + (1,) * (len(shape) - dim - 1))

    factor_of = one(*shards[0])
    for cut in shards[1:]:
        factor_of = factor_of * one(*cut)
    return factor_of


def profile(number_of, total, most, slope):
    loads = [(1 << 20) // math.isqrt(rank ** slope) + 1 for rank in range(2, number_of + 1)]
    rest, given = total - most - (number_of - 1), [1] * (number_of - 1)
    while rest > 0:
        free = [i for i in range(number_of - 1) if given[i] < most]
        whole, left = sum([loads[i] for i in free]), rest
        for i in free:
            extra = min(most - given[i], max(1, left * loads[i] // whole), rest)
            given[i] = given[i] + extra
            rest = rest - extra
    return np.array([most] + given)


def ragged_sizes(stream_key, count, total, reach, slope):
    if count == 2:
        one = jax.random.randint(stream_key, (), max(1, total - reach), min(reach, total - 1) + 1)
        return jnp.stack([one, total - one])
    tallies = jnp.asarray(profile(count, total, reach, slope), jnp.int32)
    couples = (count - 1) // 2
    source_of, sink = tallies[1:1 + 2 * couples:2], tallies[2:2 + 2 * couples:2]
    slack = jnp.minimum(source_of - 1, reach - sink)
    moved = jax.random.randint(jax.random.fold_in(stream_key, 1), (couples,), 0, 1 << 20) % (slack + 1)
    tallies = tallies.at[1:1 + 2 * couples:2].set(source_of - moved).at[2:2 + 2 * couples:2].set(sink + moved)
    return tallies[jax.random.permutation(jax.random.fold_in(stream_key, 2), count)]


def noise(rng, shape, scale, limit, pieces=(), kind=jnp.bfloat16):
    entries = jax.random.normal(rng, shape, jnp.float32) * scale
    if len(pieces) > 0:
        entries = block_levels(rng, shape, pieces, -0.22, 0.18) * entries
    return jnp.clip(entries, min=-limit, max=limit).astype(kind)


def setup_inputs(seed: int = 0) -> dict:
    keys = jax.random.split(jax.random.key(seed), 13)
    return {
        "prompt_keys": noise(keys[0], (PROMPTS * LP, KVH * HD), 1.0, 6.0, ((0, 64), (1, 8))),
        "prompt_values": noise(keys[1], (PROMPTS * LP, KVH * HD), 1.0, 6.0, ((0, 64), (1, 8))),
        "key_weight": noise(keys[2], (D, KVH * HD), D ** -0.5, 0.078125, ((0, 64), (1, 8))),
        "value_weight": noise(keys[3], (D, KVH * HD), D ** -0.5, 0.078125, ((0, 64), (1, 8))),
        "resp_query": noise(keys[4], (RESPONSES * LR, QH * HD), 1.0, 6.0, ((0, 64), (1, 8))),
        "resp_keys": noise(keys[5], (RESPONSES * LR, KVH * HD), 1.0, 6.0, ((0, 64), (1, 8))),
        "resp_values": noise(keys[6], (RESPONSES * LR, KVH * HD), 1.0, 6.0, ((0, 64), (1, 8))),
        "resp_grad": noise(keys[7], (RESPONSES * LR, QH * HD), 8.0, 48.0, ((0, 64), (1, 8))),
        "resp_lse": draw_resp_lse(jax.random.fold_in(keys[12], 71), 0),
        "resp_delta": noise(keys[9], (QH, RESPONSES * LR), 4.0, 24.0, ((0, 8), (1, 64)), jnp.float32),
        "resp_prompt": draw_resp_prompt(jax.random.fold_in(keys[12], 71), 0),
        "resp_lengths": ragged_sizes(keys[11], RESPONSES, RESPONSES * LR * 5 // 8, LR, 1).astype(jnp.int32),
    }


def attend_back(query, grad_live, log_norm, row_delta, key_rows, value_rows, key_mask):
    scaling = query.shape[-1] ** -0.5
    query_f = query.astype(jnp.float32)
    grad_f = grad_live.astype(jnp.float32)
    key_f = key_rows.astype(jnp.float32)
    value_f = value_rows.astype(jnp.float32)
    scores = jnp.einsum("crlgqd,cmgd->crlgqm", query_f, key_f) * scaling
    probs = jnp.exp(scores - log_norm[..., None])
    if key_mask is not None:
        probs = jnp.where(key_mask[:, None, None, :], probs, jnp.float32(0.0))
    probs_low = probs.astype(jnp.bfloat16)
    dprob = jnp.einsum("crlgqd,cmgd->crlgqm", grad_f, value_f)
    dscore = (probs * (dprob - row_delta[..., None])).astype(jnp.bfloat16)
    dscore_f = dscore.astype(jnp.float32)
    grad_values = jnp.einsum("crlgqm,crlgqd->cmgd", probs_low.astype(jnp.float32), grad_f)
    grad_keys = jnp.einsum("crlgqm,crlgqd->cmgd", dscore_f, query_f) * scaling
    grad_query = jnp.einsum("crlgqm,cmgd->crlgqd", dscore_f, key_f) * scaling
    return grad_query, grad_keys, grad_values


def reference(prompt_keys, prompt_values, key_weight, value_weight, resp_query, resp_keys, resp_values, resp_grad, resp_lse, resp_delta, resp_prompt, resp_lengths):
    group_heads = QH // KVH
    shaped = (PROMPTS, GROUP, LR, KVH, group_heads, HD)
    flat_shape = (RESPONSES, LR, KVH, group_heads, HD)
    valid = (jnp.arange(LR)[None, :] < resp_lengths[:, None]).reshape(PROMPTS, GROUP, LR)
    query = resp_query.reshape(shaped)
    grad_live = jnp.where(valid[..., None, None, None], resp_grad.reshape(shaped), jnp.zeros((), jnp.bfloat16))
    log_norm = resp_lse.reshape(KVH, group_heads, PROMPTS, GROUP, LR).transpose(2, 3, 4, 0, 1)
    delta_all = resp_delta.reshape(KVH, group_heads, PROMPTS, GROUP, LR).transpose(2, 3, 4, 0, 1)
    delta_live = jnp.where(valid[..., None, None], delta_all, jnp.float32(0.0))

    query_rows = query.reshape(flat_shape)
    grad_rows = grad_live.reshape(flat_shape)
    norm_rows = log_norm.reshape(RESPONSES, LR, KVH, group_heads)
    delta_rows = delta_live.reshape(RESPONSES, LR, KVH, group_heads)
    prompt_k = prompt_keys.reshape(PROMPTS, LP, KVH, HD)
    prompt_v = prompt_values.reshape(PROMPTS, LP, KVH, HD)
    by_prompt = jnp.argsort(resp_prompt, stable=True).astype(jnp.int32).reshape(PROMPTS, GROUP)

    def per_prompt(pack):
        prompt_index, members = pack
        grad_query, grad_keys, grad_values = attend_back(
            query_rows[members][None], grad_rows[members][None], norm_rows[members][None],
            delta_rows[members][None], prompt_k[prompt_index][None], prompt_v[prompt_index][None], None)
        return (grad_query[0].astype(jnp.bfloat16), grad_keys[0].astype(jnp.bfloat16),
                grad_values[0].astype(jnp.bfloat16))

    pre_dq, prompt_dk, prompt_dv = lax.map(per_prompt, (jnp.arange(PROMPTS, dtype=jnp.int32), by_prompt))
    prefix_dq = jnp.zeros(flat_shape, jnp.bfloat16).at[by_prompt.reshape(-1)].set(pre_dq.reshape(flat_shape))

    causal = jnp.arange(LR)[:, None] >= jnp.arange(LR)[None, :]
    resp_k = resp_keys.reshape(PROMPTS, GROUP, LR, KVH, HD)
    resp_v = resp_values.reshape(PROMPTS, GROUP, LR, KVH, HD)

    def per_block(pack):
        query_blk, grad_blk, norm_blk, delta_blk, key_blk, value_blk, prefix_blk = pack
        grad_query, grad_keys, grad_values = attend_back(
            query_blk[:, None], grad_blk[:, None], norm_blk[:, None], delta_blk[:, None], key_blk, value_blk, causal)
        total_dq = (grad_query[:, 0] + prefix_blk.astype(jnp.float32)).astype(jnp.bfloat16)
        return total_dq, grad_keys.astype(jnp.bfloat16), grad_values.astype(jnp.bfloat16)

    d_query, d_keys, d_values = lax.map(
        per_block, (query, grad_live, log_norm, delta_live, resp_k, resp_v, prefix_dq.reshape(shaped)))

    prompt_dk_rows = prompt_dk.reshape(PROMPTS * LP, KVH * HD)
    prompt_dv_rows = prompt_dv.reshape(PROMPTS * LP, KVH * HD)
    d_prompt_input = (jnp.dot(prompt_dk_rows, key_weight.T, preferred_element_type=jnp.float32)
                      + jnp.dot(prompt_dv_rows, value_weight.T, preferred_element_type=jnp.float32)).astype(jnp.bfloat16)
    return (d_query.reshape(RESPONSES * LR, QH * HD), d_keys.reshape(RESPONSES * LR, KVH * HD),
            d_values.reshape(RESPONSES * LR, KVH * HD), d_prompt_input)
```

```python
import math

import jax
import jax.numpy as jnp
from jax import lax
from jax.experimental import pallas as pl
from jax.experimental.pallas import tpu as pltpu
from jax.sharding import PartitionSpec as P

HD = 128
HEADS = 8
LP = 64
LR = 8
SLOTS = 16
PAIRS = SLOTS // 2
NX, NZ, NC, NY = 4, 8, 2, 8
WROWS = 80
SCALE = 1.0 / math.sqrt(HD)
MESH = pl.DeviceIdType.MESH
BF, F32 = jnp.bfloat16, jnp.float32
Z_ORDER = (4, 3, 5, 2, 6, 1, 7)
Z_NEAR = (1, 7, 2, 6, 3, 5, 4)
X_ORDER = (2, 1, 3)
Y_ORDER = (4, 3, 5, 2, 6, 1, 7)
Y_NEAR = (1, 7, 2, 6, 3, 5, 4)


def dot_nt(a, b):
    return lax.dot_general(a, b, (((1,), (1,)), ((), ())), preferred_element_type=F32)


def dot_nn(a, b):
    return lax.dot_general(a, b, (((1,), (0,)), ((), ())), preferred_element_type=F32)


def dot_tn(a, b):
    return lax.dot_general(a, b, (((0,), (0,)), ((), ())), preferred_element_type=F32)


def spread_rows(rows):
    lane = lax.broadcasted_iota(jnp.int32, (HEADS, HD), 1) // 16
    head = lax.broadcasted_iota(jnp.int32, (HEADS, HD), 0)
    turned = [rows if k == 0 else pltpu.roll(rows, 16 * k, 1) for k in range(8)]
    out = []
    for pair in range(PAIRS):
        picked = jnp.zeros((HEADS, HD), F32)
        for h in range(HEADS):
            picked = jnp.where((head == h) & (lane == h), turned[(h - pair) % 8], picked)
        out.append(jnp.sum(picked, axis=0, keepdims=True))
    return jnp.concatenate(out, axis=0)


def kernel(
    pk_ref, pv_ref, kw_ref, vw_ref, q_ref, rk_ref, rv_ref, g_ref, lse_ref, delta_ref, prompt_ref, len_ref,
    dq_ref, drk_ref, drv_ref, out_ref,
    kv, wst, wbuf, q, g, rk, rv, lse, delta, lse_t, delta_t,
    own, sib, table, table_s, snd1, rcv1, snd2, rcv2, rcv3,
    load_sem, table_sem,
    kz_s, kz_r, kx_s, kx_r, kc_s, kc_r,
    w0_s, w0_r, wx_s, wx_r, wz_s, wz_r, wc_s, wc_r,
    rc_s, rc_r, rx_s, rx_r, rz_s, rz_r, ry_s, ry_r,
):
    me = lax.axis_index("dp")
    t = lax.axis_index("tensor")
    x, z, c = me // 16, (me // 2) % 8, me % 2

    def at(xx, zz, cc):
        return xx * 16 + zz * 2 + cc

    def xp(k):
        return (at((x + k) % NX, z, c), t)

    def zp(k):
        return (at(x, (z + k) % NZ, c), t)

    def yp(k):
        return (me, (t + k) % NY)

    other = (at(x, z, 1 - c), t)

    def remote(src, dst, s, r, dev):
        return pltpu.make_async_remote_copy(src_ref=src, dst_ref=dst, send_sem=s, recv_sem=r, device_id=dev, device_id_type=MESH)

    loads = [
        (pk_ref, kv.at[me, 0:LP]),
        (pv_ref, kv.at[me, LP : 2 * LP]),
        (kw_ref, wst.at[0:WROWS]),
        (vw_ref, wst.at[WROWS : 2 * WROWS]),
        (q_ref, q),
        (g_ref, g),
        (rk_ref, rk),
        (rv_ref, rv),
        (lse_ref, lse),
        (delta_ref, delta),
    ]
    loads = [pltpu.make_async_copy(a, b, load_sem.at[i]) for i, (a, b) in enumerate(loads)]
    for copy in loads:
        copy.start()

    w_to = (at((me % 4 + 1) % NX, t, (me // 4) % 2), me // 8)
    w_from = (8 * t + 4 * c + (x + 3) % 4, z)

    barrier = pltpu.get_barrier_semaphore()
    peers = [zp(k) for k in range(1, NZ)] + [xp(k) for k in range(1, NX)] + [yp(k) for k in range(1, NY)]
    peers += [other, w_to, w_from]
    for dev in peers:
        pl.semaphore_signal(barrier, inc=1, device_id=dev, device_id_type=MESH)
    loads[0].wait()
    loads[1].wait()
    loads[2].wait()
    loads[3].wait()
    pl.semaphore_wait(barrier, len(peers))

    sent = []

    def go(copy):
        copy.start()
        sent.append(copy)

    def kz(k):
        return remote(kv.at[me], kv.at[me], kz_s.at[k], kz_r.at[k], zp(k))

    def from_z(k):
        return at(x, (z - k + NZ) % NZ, c)

    def kx(kz_, k):
        p = from_z(kz_)
        return remote(kv.at[p], kv.at[p], kx_s.at[kz_, k], kx_r.at[kz_, k], xp(k))

    def kc(kz_, k):
        p = at((x - k + NX) % NX, (z - kz_ + NZ) % NZ, c)
        return remote(kv.at[p], kv.at[p], kc_s.at[kz_, k], kc_r.at[kz_, k], other)

    def kc_in(kz_, k):
        p = at((x - k + NX) % NX, (z - kz_ + NZ) % NZ, 1 - c)
        return remote(kv.at[p], kv.at[p], kc_s.at[kz_, k], kc_r.at[kz_, k], other)

    def kz_in(k):
        p = from_z(k)
        return remote(kv.at[p], kv.at[p], kz_s.at[k], kz_r.at[k], zp(k))

    def kx_in(kz_, k):
        p = at((x - k + NX) % NX, (z - kz_ + NZ) % NZ, c)
        return remote(kv.at[p], kv.at[p], kx_s.at[kz_, k], kx_r.at[kz_, k], xp(k))

    for k in Z_ORDER:
        go(kz(k))
    for k in X_ORDER:
        go(kx(0, k))
    go(kc(0, 0))

    wt_x, wt_z, wt_c = (me % 4 + 1) % NX, t, (me // 4) % 2
    go(remote(wst, wbuf.at[wt_c, wt_z, wt_x], w0_s, w0_r, w_to))

    lane = lax.broadcasted_iota(jnp.int32, (1, HD), 1)
    rows = []
    for base in (me, at(x, z, 1 - c)):
        found = jnp.full((1, HD), SLOTS, jnp.int32)
        for s in range(SLOTS):
            found = jnp.where(lane == prompt_ref[base * SLOTS + s], s, found)
        rows.append(found)
    table[0:1, :] = rows[0]
    table[1:2, :] = rows[1]
    table_copy = pltpu.make_async_copy(table, table_s, table_sem)
    table_copy.start()
    own[SLOTS] = jnp.zeros((2 * LP, HD), BF)
    sib[SLOTS] = jnp.zeros((2 * LP, HD), BF)

    for copy in loads[4:]:
        copy.wait()
    lse_t[...] = spread_rows(lse[...])
    delta_t[...] = spread_rows(delta[...])

    for k in Z_NEAR:
        kz_in(k).wait_recv()
        for k2 in X_ORDER:
            go(kx(k, k2))
        go(kc(k, 0))

    w_mine = remote(wst, wbuf.at[c, z, x], w0_s, w0_r, w_to)
    w_mine.wait_recv()

    def wx(k):
        return remote(wbuf.at[c, z, x], wbuf.at[c, z, x], wx_s.at[k], wx_r.at[k], xp(k))

    def wx_in(k):
        xx = (x - k + NX) % NX
        return remote(wbuf.at[c, z, xx], wbuf.at[c, z, xx], wx_s.at[k], wx_r.at[k], xp(k))

    for k in X_ORDER:
        go(wx(k))

    for k in (0,) + Z_NEAR:
        for k2 in (1, 3, 2):
            kx_in(k, k2).wait_recv()
            go(kc(k, k2))

    def wz(k, way):
        zz = (z - (k - 1) * way + NZ) % NZ
        return remote(wbuf.at[c, zz], wbuf.at[c, zz], wz_s.at[(k * way) % NZ], wz_r.at[(k * way) % NZ], zp(way % NZ))

    def wz_in(k, way):
        zz = (z - k * way + NZ) % NZ
        return remote(wbuf.at[c, zz], wbuf.at[c, zz], wz_s.at[(k * way) % NZ], wz_r.at[(k * way) % NZ], zp(way % NZ))

    def wc(k):
        zz = (z - k + NZ) % NZ
        return remote(wbuf.at[c, zz], wbuf.at[c, zz], wc_s.at[k], wc_r.at[k], other)

    def wc_in(k):
        zz = (z - k + NZ) % NZ
        return remote(wbuf.at[1 - c, zz], wbuf.at[1 - c, zz], wc_s.at[k], wc_r.at[k], other)

    def w_hop(k):
        for way in (1, -1):
            if k > 1 and (way == 1 or k <= 4):
                wz_in(k - 1, way).wait_recv()
        for way in (1, -1):
            if k <= (4 if way == 1 else 3):
                go(wz(k, way))
        if k == 1:
            go(wc(0))
        else:
            for way in (1, -1):
                if way == 1 or k <= 4:
                    go(wc(((k - 1) * way) % NZ))

    for k in X_ORDER:
        wx_in(k).wait_recv()
    w_hop(1)

    for k in range(NZ):
        for k2 in range(NX):
            kc_in(k, k2).wait_recv()

    key_row = lax.broadcasted_iota(jnp.int32, (2 * LP + 16, HD), 0)
    column = lax.broadcasted_iota(jnp.int32, (2 * LP + 16, HD), 1)
    col_r, col_t = (column // LR) % 2, column % LR
    in_own = key_row >= 2 * LP
    row_r = jnp.where(in_own, (key_row - 2 * LP) // LR, key_row // LP)
    seen = (row_r == col_r) & (jnp.logical_not(in_own) | ((key_row % LR) <= col_t))
    col_r1, col_t1 = col_r[0:1], col_t[0:1]

    def one_pair(pair):
        base = pl.multiple_of(pair * 16, 16)
        p0, p1 = prompt_ref[me * SLOTS + 2 * pair], prompt_ref[me * SLOTS + 2 * pair + 1]
        l0, l1 = len_ref[2 * pair], len_ref[2 * pair + 1]
        kv0, kv1 = kv[p0], kv[p1]
        keys = jnp.concatenate([kv0[:LP], kv1[:LP], rk[pl.ds(base, 16)]], axis=0)
        values = jnp.concatenate([kv0[LP:], kv1[LP:], rv[pl.ds(base, 16)]], axis=0)
        qp = jnp.concatenate([q[pl.ds(base, 16), h * HD : (h + 1) * HD] for h in range(HEADS)], axis=0)
        gp = jnp.concatenate([g[pl.ds(base, 16), h * HD : (h + 1) * HD] for h in range(HEADS)], axis=0)
        live = col_t1 < jnp.where(col_r1 == 0, l0, l1)
        scores = dot_nt(keys, qp) * SCALE
        probs = jnp.exp(scores - lse_t[pl.ds(pair, 1)])
        probs = jnp.where(seen & live, probs, 0.0)
        dprob = dot_nt(values, gp)
        dscore = (probs * (dprob - delta_t[pl.ds(pair, 1)])).astype(BF)
        dv = dot_nn(probs.astype(BF), gp)
        dk = dot_nn(dscore, qp)
        dq = dot_tn(dscore, keys) * SCALE
        for r in range(2):
            own[2 * pair + r, 0:LP] = dk[r * LP : (r + 1) * LP].astype(BF)
            own[2 * pair + r, LP : 2 * LP] = dv[r * LP : (r + 1) * LP].astype(BF)
        drk_ref[pl.ds(base, 16)] = (dk[2 * LP :] * SCALE).astype(BF)
        drv_ref[pl.ds(base, 16)] = dv[2 * LP :].astype(BF)
        for h in range(HEADS):
            dq_ref[pl.ds(base, 16), h * HD : (h + 1) * HD] = dq[h * 16 : (h + 1) * 16].astype(BF)

    def rc(i):
        return remote(own.at[pl.ds(4 * i, 4)], sib.at[pl.ds(4 * i, 4)], rc_s.at[i], rc_r.at[i], other)

    for i in range(4):
        one_pair(2 * i)
        one_pair(2 * i + 1)
        go(rc(i))
        if i == 1:
            w_hop(2)
        if i == 3:
            w_hop(3)

    table_copy.wait()
    for i in range(4):
        rc(i).wait_recv()

    def both_cores(j):
        return own[table_s[0, j]].astype(F32) + sib[table_s[1, j]].astype(F32)

    def rx(k, half):
        part = pl.ds(4 * half, 4)
        return remote(snd1.at[k - 1, part], rcv1.at[k - 1, part], rx_s.at[k - 1, half], rx_r.at[k - 1, half], xp(k))

    ranks = Z_ORDER + (0,)
    for half in range(2):
        for k in X_ORDER:
            for i in range(4 * half, 4 * half + 4):
                j = at((x + k) % NX, (z + ranks[i]) % NZ, c)
                snd1[k - 1, i] = both_cores(j).astype(BF)
            go(rx(k, half))

    def rz(i):
        k = ranks[i]
        return remote(snd2.at[i], rcv2.at[i], rz_s.at[i], rz_r.at[i], zp(k))

    w_hop(4)
    mine = None
    for half in range(2):
        for k in X_ORDER:
            rx(k, half).wait_recv()
        for i in range(4 * half, 4 * half + 4):
            total = both_cores(at(x, (z + ranks[i]) % NZ, c))
            for k in range(NX - 1):
                total = total + rcv1[k, i].astype(F32)
            if i < NZ - 1:
                snd2[i] = total.astype(BF)
                go(rz(i))
            else:
                mine = total
    wz_in(4, 1).wait_recv()
    go(wc(4))
    for i in range(NZ - 1):
        rz(i).wait_recv()
        mine = mine + rcv2[i].astype(F32)
    row = lax.broadcasted_iota(jnp.int32, (2 * LP, HD), 0)
    rcv3[0] = jnp.where(row < LP, mine * SCALE, mine).astype(BF)

    def ry(k):
        return remote(rcv3.at[0], rcv3.at[k], ry_s.at[k], ry_r.at[k], yp(k))

    for k in Y_ORDER:
        go(ry(k))
    for k in range(NZ):
        wc_in(k).wait_recv()

    def project(k):
        head = (t - k + NY) % NY
        part = rcv3[k]
        both = jnp.concatenate([part[:LP], part[LP:]], axis=1)
        weights = []
        for cc in range(NC):
            for j in range(4):
                block = wbuf[cc, head, (j + 1) % 4]
                weights.append(jnp.concatenate([block[:WROWS], block[WROWS:]], axis=1))
        return dot_nt(both, jnp.concatenate(weights, axis=0))

    acc = project(0)
    for k in Y_NEAR:
        ry(k).wait_recv()
        acc = acc + project(k)
    out_ref[...] = acc.astype(BF)

    for copy in sent:
        copy.wait_send()


def body(*args):
    vmem = pl.BlockSpec(memory_space=pltpu.VMEM)
    smem = pl.BlockSpec(memory_space=pltpu.SMEM)
    hbm = pl.BlockSpec(memory_space=pl.ANY)
    rows = SLOTS * LR
    dma = pltpu.SemaphoreType.DMA
    return pl.pallas_call(
        kernel,
        out_shape=(
            jax.ShapeDtypeStruct((rows, HEADS * HD), BF),
            jax.ShapeDtypeStruct((rows, HD), BF),
            jax.ShapeDtypeStruct((rows, HD), BF),
            jax.ShapeDtypeStruct((LP, 8 * WROWS), BF),
        ),
        in_specs=[hbm] * 10 + [smem] * 2,
        out_specs=(vmem,) * 4,
        scratch_shapes=[
            pltpu.VMEM((64, 2 * LP, HD), BF),
            pltpu.VMEM((2 * WROWS, HD), BF),
            pltpu.VMEM((NC, NZ, NX, 2 * WROWS, HD), BF),
            pltpu.VMEM((rows, HEADS * HD), BF),
            pltpu.VMEM((rows, HEADS * HD), BF),
            pltpu.VMEM((rows, HD), BF),
            pltpu.VMEM((rows, HD), BF),
            pltpu.VMEM((HEADS, rows), F32),
            pltpu.VMEM((HEADS, rows), F32),
            pltpu.VMEM((PAIRS, HD), F32),
            pltpu.VMEM((PAIRS, HD), F32),
            pltpu.VMEM((SLOTS + 1, 2 * LP, HD), BF),
            pltpu.VMEM((SLOTS + 1, 2 * LP, HD), BF),
            pltpu.VMEM((8, HD), jnp.int32),
            pltpu.SMEM((8, HD), jnp.int32),
            pltpu.VMEM((NX - 1, NZ, 2 * LP, HD), BF),
            pltpu.VMEM((NX - 1, NZ, 2 * LP, HD), BF),
            pltpu.VMEM((NZ - 1, 2 * LP, HD), BF),
            pltpu.VMEM((NZ - 1, 2 * LP, HD), BF),
            pltpu.VMEM((NY, 2 * LP, HD), BF),
            dma((10,)),
            dma,
            dma((NZ,)), dma((NZ,)), dma((NZ, NX)), dma((NZ, NX)), dma((NZ, NX)), dma((NZ, NX)),
            dma, dma, dma((NX,)), dma((NX,)), dma((NZ,)), dma((NZ,)), dma((NZ,)), dma((NZ,)),
            dma((4,)), dma((4,)), dma((NX - 1, 2)), dma((NX - 1, 2)), dma((NZ,)), dma((NZ,)), dma((NY,)), dma((NY,)),
        ],
        compiler_params=pltpu.CompilerParams(
            collective_id=0, has_side_effects=True, vmem_limit_bytes=32 << 20
        ),
        name="attention_back",
    )(*args)


def solution(mesh):
    split = P("dp", "tensor")
    return jax.shard_map(
        body,
        mesh=mesh,
        in_specs=(split,) * 8 + (P("tensor", "dp"),) * 2 + (P(), P("dp")),
        out_specs=(split,) * 4,
        check_vma=False,
    )
```

```python
import math

import jax
import jax.numpy as jnp
from jax import lax
from jax.experimental import pallas as pl
from jax.experimental.pallas import tpu as pltpu
from jax.sharding import PartitionSpec as P

HD = 128
HEADS = 8
LP = 64
LR = 8
SLOTS = 16
PAIRS = SLOTS // 2
NX, NZ, NC, NY = 4, 8, 2, 8
WROWS = 80
SCALE = 1.0 / math.sqrt(HD)
MESH = pl.DeviceIdType.MESH
BF, F32 = jnp.bfloat16, jnp.float32
Z_RANKS = (0, 1, 7, 2, 6, 3, 5, 4)
Z_FAR = Z_RANKS[:0:-1]
X_ORDER = (2, 1, 3)
Y_ORDER = (4, 3, 5, 2, 6, 1, 7)
Y_NEAR = (1, 7, 2, 6, 3, 5, 4)


def dot_nt(a, b):
    return lax.dot_general(a, b, (((1,), (1,)), ((), ())), preferred_element_type=F32)


def dot_nn(a, b):
    return lax.dot_general(a, b, (((1,), (0,)), ((), ())), preferred_element_type=F32)


def dot_tn(a, b):
    return lax.dot_general(a, b, (((0,), (0,)), ((), ())), preferred_element_type=F32)


def rank(k):
    return jnp.where(k == 0, 0, jnp.where(k <= 4, 2 * k - 1, 16 - 2 * k))


def spread_rows(rows):
    lane = lax.broadcasted_iota(jnp.int32, (HEADS, HD), 1) // 16
    head = lax.broadcasted_iota(jnp.int32, (HEADS, HD), 0)
    turned = [rows if k == 0 else pltpu.roll(rows, 16 * k, 1) for k in range(8)]
    out = []
    for pair in range(PAIRS):
        picked = jnp.zeros((HEADS, HD), F32)
        for h in range(HEADS):
            picked = jnp.where((head == h) & (lane == h), turned[(h - pair) % 8], picked)
        out.append(jnp.sum(picked, axis=0, keepdims=True))
    return jnp.concatenate(out, axis=0)


def kernel(
    pk_ref, pv_ref, kw_ref, vw_ref, q_ref, rk_ref, rv_ref, g_ref, lse_ref, delta_ref, prompt_in, len_in,
    dq_ref, drk_ref, drv_ref, out_ref,
    prompt_ref, len_ref, kv, wst, wbuf, q, g, rk, rv, lse, delta, lse_t, delta_t,
    own, sib, table, table_s, snd1, rcv1, snd2, rcv2, rcv3,
    load_sem, table_sem,
    kz_s, kz_r, kx_s, kx_r, kc_s, kc_r,
    w0_s, w0_r, wx_s, wx_r, wz_s, wz_r, wc_s, wc_r,
    rc_s, rc_r, rx_s, rx_r, rz_s, rz_r, ry_s, ry_r,
):
    me = lax.axis_index("dp")
    t = lax.axis_index("tensor")
    x, z, c = me // 16, (me // 2) % 8, me % 2

    def at(xx, zz, cc):
        return xx * 16 + zz * 2 + cc

    def xp(k):
        return (at((x + k) % NX, z, c), t)

    def zp(k):
        return (at(x, (z + k) % NZ, c), t)

    def yp(k):
        return (me, (t + k) % NY)

    other = (at(x, z, 1 - c), t)

    def remote(src, dst, s, r, dev):
        return pltpu.make_async_remote_copy(src_ref=src, dst_ref=dst, send_sem=s, recv_sem=r, device_id=dev, device_id_type=MESH)

    loads = [
        (pk_ref, kv.at[c, x, 0, 0:LP]),
        (pv_ref, kv.at[c, x, 0, LP : 2 * LP]),
        (kw_ref, wst.at[0:WROWS]),
        (vw_ref, wst.at[WROWS : 2 * WROWS]),
        (q_ref, q),
        (g_ref, g),
        (rk_ref, rk),
        (rv_ref, rv),
        (lse_ref, lse),
        (delta_ref, delta),
        (prompt_in, prompt_ref),
        (len_in, len_ref),
    ]
    loads = [pltpu.make_async_copy(a, b, load_sem.at[i]) for i, (a, b) in enumerate(loads)]
    for copy in loads:
        copy.start()

    w_to = (at((me % 4 + 1) % NX, t, (me // 4) % 2), me // 8)
    w_from = (8 * t + 4 * c + (x + 3) % 4, z)

    barrier = pltpu.get_barrier_semaphore()
    peers = [zp(k) for k in range(1, NZ)] + [xp(k) for k in range(1, NX)] + [yp(k) for k in range(1, NY)]
    peers += [other, w_to, w_from]
    for dev in peers:
        pl.semaphore_signal(barrier, inc=1, device_id=dev, device_id_type=MESH)
    loads[0].wait()
    loads[1].wait()
    loads[2].wait()
    loads[3].wait()
    pl.semaphore_wait(barrier, len(peers))

    sent = []

    def go(copy):
        copy.start()
        sent.append(copy)

    wt_c, wt_z, wt_x = (me // 4) % 2, t, (me % 4 + 1) % NX

    def wz(i):
        return remote(wbuf.at[c, x, 0], wbuf.at[c, x, i], wz_s.at[i], wz_r.at[i], zp(Z_RANKS[i]))

    def wx(k):
        return remote(wbuf.at[c, x], wbuf.at[c, x], wx_s.at[k], wx_r.at[k], xp(k))

    def wx_in(k):
        dst = wbuf.at[c, (x - k + NX) % NX]
        return remote(dst, dst, wx_s.at[k], wx_r.at[k], xp(k))

    def wc(k):
        group = wbuf.at[c, (x - k + NX) % NX]
        return remote(group, group, wc_s.at[k], wc_r.at[k], other)

    def wc_in(k):
        group = wbuf.at[1 - c, (x - k + NX) % NX]
        return remote(group, group, wc_s.at[k], wc_r.at[k], other)

    def weights(step):
        if step == 0:
            go(remote(wst, wbuf.at[wt_c, wt_x, 0], w0_s, w0_r, w_to))
        elif step == 1:
            remote(wst, wbuf.at[c, x, 0], w0_s, w0_r, w_to).wait_recv()
            for i in range(NZ - 1, 0, -1):
                go(wz(i))
        elif step == 2:
            for i in range(1, NZ):
                wz(i).wait_recv()
            for k in X_ORDER:
                go(wx(k))
            go(wc(0))
        elif step == 3:
            for k in (1, 3, 2):
                wx_in(k).wait_recv()
                go(wc(k))
        else:
            for k in range(NX):
                wc_in(k).wait_recv()

    def kz(i):
        return remote(kv.at[c, x, 0], kv.at[c, x, i], kz_s.at[i], kz_r.at[i], zp(Z_RANKS[i]))

    def half_of(cc, xx, half):
        return kv.at[cc, xx, pl.ds(4 * half, 4)]

    def kx(k, half):
        group = half_of(c, x, half)
        return remote(group, group, kx_s.at[k, half], kx_r.at[k, half], xp(k))

    def kx_in(k, half):
        group = half_of(c, (x - k + NX) % NX, half)
        return remote(group, group, kx_s.at[k, half], kx_r.at[k, half], xp(k))

    def kc(k, half):
        group = half_of(c, (x - k + NX) % NX, half)
        return remote(group, group, kc_s.at[k, half], kc_r.at[k, half], other)

    def kc_in(k, half):
        group = half_of(1 - c, (x - k + NX) % NX, half)
        return remote(group, group, kc_s.at[k, half], kc_r.at[k, half], other)

    for i in range(NZ - 1, 0, -1):
        go(kz(i))
    weights(0)

    for copy in loads[4:]:
        copy.wait()

    lane = lax.broadcasted_iota(jnp.int32, (1, HD), 1)
    rows = []
    for base in (me, at(x, z, 1 - c)):
        found = jnp.full((1, HD), SLOTS, jnp.int32)
        for s in range(SLOTS):
            found = jnp.where(lane == prompt_ref[base * SLOTS + s], s, found)
        rows.append(found)
    table[0:1, :] = rows[0]
    table[1:2, :] = rows[1]
    table_copy = pltpu.make_async_copy(table, table_s, table_sem)
    table_copy.start()
    own[SLOTS] = jnp.zeros((2 * LP, HD), BF)
    sib[SLOTS] = jnp.zeros((2 * LP, HD), BF)

    lse_t[...] = spread_rows(lse[...])
    delta_t[...] = spread_rows(delta[...])

    for half in range(2):
        for i in range(max(4 * half, 1), 4 * half + 4):
            kz(i).wait_recv()
        for k in X_ORDER:
            go(kx(k, half))
        go(kc(0, half))
    weights(1)
    for half in range(2):
        for k in (1, 3, 2):
            kx_in(k, half).wait_recv()
            go(kc(k, half))
    for half in range(2):
        for k in range(NX):
            kc_in(k, half).wait_recv()

    key_row = lax.broadcasted_iota(jnp.int32, (2 * LP + 16, HD), 0)
    column = lax.broadcasted_iota(jnp.int32, (2 * LP + 16, HD), 1)
    col_r, col_t = (column // LR) % 2, column % LR
    in_own = key_row >= 2 * LP
    row_r = jnp.where(in_own, (key_row - 2 * LP) // LR, key_row // LP)
    seen = (row_r == col_r) & (jnp.logical_not(in_own) | ((key_row % LR) <= col_t))
    col_r1, col_t1 = col_r[0:1], col_t[0:1]

    def one_pair(pair):
        base = pl.multiple_of(pair * 16, 16)
        p0, p1 = prompt_ref[me * SLOTS + 2 * pair], prompt_ref[me * SLOTS + 2 * pair + 1]
        l0, l1 = len_ref[2 * pair], len_ref[2 * pair + 1]
        kv0, kv1 = (kv[p % 2, p // 16, rank((z - (p // 2) % 8 + NZ) % NZ)] for p in (p0, p1))
        keys = jnp.concatenate([kv0[:LP], kv1[:LP], rk[pl.ds(base, 16)]], axis=0)
        values = jnp.concatenate([kv0[LP:], kv1[LP:], rv[pl.ds(base, 16)]], axis=0)
        qp = jnp.concatenate([q[pl.ds(base, 16), h * HD : (h + 1) * HD] for h in range(HEADS)], axis=0)
        gp = jnp.concatenate([g[pl.ds(base, 16), h * HD : (h + 1) * HD] for h in range(HEADS)], axis=0)
        live = col_t1 < jnp.where(col_r1 == 0, l0, l1)
        scores = dot_nt(keys, qp) * SCALE
        probs = jnp.exp(scores - lse_t[pl.ds(pair, 1)])
        probs = jnp.where(seen & live, probs, 0.0)
        dprob = dot_nt(values, gp)
        dscore = (probs * (dprob - delta_t[pl.ds(pair, 1)])).astype(BF)
        dv = dot_nn(probs.astype(BF), gp)
        dk = dot_nn(dscore, qp)
        dq = dot_tn(dscore, keys) * SCALE
        for r in range(2):
            own[2 * pair + r, 0:LP] = dk[r * LP : (r + 1) * LP].astype(BF)
            own[2 * pair + r, LP : 2 * LP] = dv[r * LP : (r + 1) * LP].astype(BF)
        drk_ref[pl.ds(base, 16)] = (dk[2 * LP :] * SCALE).astype(BF)
        drv_ref[pl.ds(base, 16)] = dv[2 * LP :].astype(BF)
        for h in range(HEADS):
            dq_ref[pl.ds(base, 16), h * HD : (h + 1) * HD] = dq[h * 16 : (h + 1) * 16].astype(BF)

    def rc(i):
        return remote(own.at[pl.ds(4 * i, 4)], sib.at[pl.ds(4 * i, 4)], rc_s.at[i], rc_r.at[i], other)

    for i in range(4):
        one_pair(2 * i)
        one_pair(2 * i + 1)
        go(rc(i))
        if i == 1:
            weights(2)

    table_copy.wait()
    for i in range(4):
        rc(i).wait_recv()

    def both_cores(j, part):
        rows = slice(LP * part, LP * (part + 1))
        return own[table_s[0, j], rows].astype(F32) + sib[table_s[1, j], rows].astype(F32)

    def rx(k, part):
        return remote(snd1.at[part, k - 1], rcv1.at[part, k - 1], rx_s.at[part, k - 1], rx_r.at[part, k - 1], xp(k))

    def rz(i, part):
        return remote(snd2.at[part, i], rcv2.at[part, i], rz_s.at[part, i], rz_r.at[part, i], zp(Z_RANKS[i]))

    def ry(k, part):
        rows = pl.ds(LP * part, LP)
        return remote(rcv3.at[0, rows], rcv3.at[k, rows], ry_s.at[part, k], ry_r.at[part, k], yp(k))

    def ahead(i):
        return (z + Z_RANKS[i]) % NZ

    for part in range(2):
        for k in X_ORDER:
            for i in range(NZ):
                snd1[part, k - 1, i] = both_cores(at((x + k) % NX, ahead(i), c), part).astype(BF)
            go(rx(k, part))

    mine = [None, None]
    for part in range(2):
        for k in (1, 3, 2):
            rx(k, part).wait_recv()
        for i in range(NZ - 1, -1, -1):
            total = both_cores(at(x, ahead(i), c), part)
            for k in range(NX - 1):
                total = total + rcv1[part, k, i].astype(F32)
            if i:
                snd2[part, i] = total.astype(BF)
                go(rz(i, part))
            else:
                mine[part] = total
    weights(3)
    for part in range(2):
        for i in range(1, NZ):
            rz(i, part).wait_recv()
            mine[part] = mine[part] + rcv2[part, i].astype(F32)
        rcv3[0, LP * part : LP * (part + 1)] = (mine[part] * SCALE if part == 0 else mine[part]).astype(BF)
        for k in Y_ORDER:
            go(ry(k, part))
    weights(4)

    def project(k):
        head = (t - k + NY) % NY
        place = rank((z - head + NZ) % NZ)
        grads = rcv3[k]
        both = jnp.concatenate([grads[:LP], grads[LP:]], axis=1)
        weights = []
        for cc in range(NC):
            for j in range(4):
                block = wbuf[cc, (j + 1) % NX, place]
                weights.append(jnp.concatenate([block[:WROWS], block[WROWS:]], axis=1))
        return dot_nt(both, jnp.concatenate(weights, axis=0))

    acc = project(0)
    for k in Y_NEAR:
        for part in range(2):
            ry(k, part).wait_recv()
        acc = acc + project(k)
    out_ref[...] = acc.astype(BF)

    for copy in sent:
        copy.wait_send()


def body(*args):
    vmem = pl.BlockSpec(memory_space=pltpu.VMEM)
    hbm = pl.BlockSpec(memory_space=pl.ANY)
    rows = SLOTS * LR
    dma = pltpu.SemaphoreType.DMA
    return pl.pallas_call(
        kernel,
        out_shape=(
            jax.ShapeDtypeStruct((rows, HEADS * HD), BF),
            jax.ShapeDtypeStruct((rows, HD), BF),
            jax.ShapeDtypeStruct((rows, HD), BF),
            jax.ShapeDtypeStruct((LP, 8 * WROWS), BF),
        ),
        in_specs=[hbm] * 12,
        out_specs=(vmem,) * 4,
        scratch_shapes=[
            pltpu.SMEM((64 * SLOTS,), jnp.int32),
            pltpu.SMEM((SLOTS,), jnp.int32),
            pltpu.VMEM((NC, NX, NZ, 2 * LP, HD), BF),
            pltpu.VMEM((2 * WROWS, HD), BF),
            pltpu.VMEM((NC, NX, NZ, 2 * WROWS, HD), BF),
            pltpu.VMEM((rows, HEADS * HD), BF),
            pltpu.VMEM((rows, HEADS * HD), BF),
            pltpu.VMEM((rows, HD), BF),
            pltpu.VMEM((rows, HD), BF),
            pltpu.VMEM((HEADS, rows), F32),
            pltpu.VMEM((HEADS, rows), F32),
            pltpu.VMEM((PAIRS, HD), F32),
            pltpu.VMEM((PAIRS, HD), F32),
            pltpu.VMEM((SLOTS + 1, 2 * LP, HD), BF),
            pltpu.VMEM((SLOTS + 1, 2 * LP, HD), BF),
            pltpu.VMEM((8, HD), jnp.int32),
            pltpu.SMEM((8, HD), jnp.int32),
            pltpu.VMEM((2, NX - 1, NZ, LP, HD), BF),
            pltpu.VMEM((2, NX - 1, NZ, LP, HD), BF),
            pltpu.VMEM((2, NZ, LP, HD), BF),
            pltpu.VMEM((2, NZ, LP, HD), BF),
            pltpu.VMEM((NY, 2 * LP, HD), BF),
            dma((12,)),
            dma,
            dma((NZ,)), dma((NZ,)), dma((NX, 2)), dma((NX, 2)), dma((NX, 2)), dma((NX, 2)),
            dma, dma, dma((NX,)), dma((NX,)), dma((NZ,)), dma((NZ,)), dma((NX,)), dma((NX,)),
            dma((4,)), dma((4,)), dma((2, NX - 1)), dma((2, NX - 1)), dma((2, NZ)), dma((2, NZ)), dma((2, NY)), dma((2, NY)),
        ],
        compiler_params=pltpu.CompilerParams(
            collective_id=0, has_side_effects=True, vmem_limit_bytes=62 << 20
        ),
        name="attention_back",
    )(*args)


def solution(mesh):
    split = P("dp", "tensor")
    return jax.shard_map(
        body,
        mesh=mesh,
        in_specs=(split,) * 8 + (P("tensor", "dp"),) * 2 + (P(), P("dp")),
        out_specs=(split,) * 4,
        check_vma=False,
    )
```

```python
import math

import jax
import jax.numpy as jnp
from jax import lax
from jax.experimental import pallas as pl
from jax.experimental.pallas import tpu as pltpu
from jax.sharding import PartitionSpec as P

HD = 128
HEADS = 8
LP = 64
LR = 8
SLOTS = 16
PAIRS = SLOTS // 2
NX, NZ, NC, NY = 4, 8, 2, 8
WROWS = 80
SCALE = 1.0 / math.sqrt(HD)
MESH = pl.DeviceIdType.MESH
BF, F32 = jnp.bfloat16, jnp.float32
Z_RANKS = (0, 1, 7, 2, 6, 3, 5, 4)
Z_GROUPS = ((0, 1), (1, 2), (3, 2), (5, 2), (7, 1))
GO_RIGHT = (0, 1, 4)
Y_ORDER = (4, 3, 5, 2, 6, 1, 7)
Y_NEAR = (1, 7, 2, 6, 3, 5, 4)


def dot_nt(a, b):
    return lax.dot_general(a, b, (((1,), (1,)), ((), ())), preferred_element_type=F32)


def dot_nn(a, b):
    return lax.dot_general(a, b, (((1,), (0,)), ((), ())), preferred_element_type=F32)


def dot_tn(a, b):
    return lax.dot_general(a, b, (((0,), (0,)), ((), ())), preferred_element_type=F32)


def rank(k):
    return jnp.where(k == 0, 0, jnp.where(k <= 4, 2 * k - 1, 16 - 2 * k))


def spread_rows(rows):
    lane = lax.broadcasted_iota(jnp.int32, (HEADS, HD), 1) // 16
    head = lax.broadcasted_iota(jnp.int32, (HEADS, HD), 0)
    turned = [rows if k == 0 else pltpu.roll(rows, 16 * k, 1) for k in range(8)]
    out = []
    for pair in range(PAIRS):
        picked = jnp.zeros((HEADS, HD), F32)
        for h in range(HEADS):
            picked = jnp.where((head == h) & (lane == h), turned[(h - pair) % 8], picked)
        out.append(jnp.sum(picked, axis=0, keepdims=True))
    return jnp.concatenate(out, axis=0)


def kernel(
    pk_ref, pv_ref, kw_ref, vw_ref, q_ref, rk_ref, rv_ref, g_ref, lse_ref, delta_ref, prompt_in, len_in,
    dq_ref, drk_ref, drv_ref, out_ref,
    prompt_ref, len_ref, kv, wst, wbuf, q, g, rk, rv, lse, delta, lse_t, delta_t,
    own, sib, table, table_s, snd0, rcv0, snd1, rcv1, snd2, rcv2, rcv3,
    load_sem, table_sem,
    kv_s, kv_r, w0_s, w0_r, wg_s, wg_r,
    rc_s, rc_r, rf_s, rf_r, rn_s, rn_r, rz_s, rz_r, ry_s, ry_r,
):
    me = lax.axis_index("dp")
    t = lax.axis_index("tensor")
    x, z, c = me // 16, (me // 2) % 8, me % 2

    def at(xx, zz, cc):
        return xx * 16 + zz * 2 + cc

    def xp(k):
        return (at((x + k) % NX, z, c), t)

    def zp(k):
        return (at(x, (z + k) % NZ, c), t)

    def yp(k):
        return (me, (t + k) % NY)

    other = (at(x, z, 1 - c), t)

    def remote(src, dst, s, r, dev):
        return pltpu.make_async_remote_copy(src_ref=src, dst_ref=dst, send_sem=s, recv_sem=r, device_id=dev, device_id_type=MESH)

    loads = [
        (pk_ref, kv.at[c, x, 0, 0:LP]),
        (pv_ref, kv.at[c, x, 0, LP : 2 * LP]),
        (kw_ref, wst.at[0:WROWS]),
        (vw_ref, wst.at[WROWS : 2 * WROWS]),
        (q_ref, q),
        (g_ref, g),
        (rk_ref, rk),
        (rv_ref, rv),
        (lse_ref, lse),
        (delta_ref, delta),
        (prompt_in, prompt_ref),
        (len_in, len_ref),
    ]
    loads = [pltpu.make_async_copy(a, b, load_sem.at[i]) for i, (a, b) in enumerate(loads)]
    for copy in loads:
        copy.start()

    w_to = (at((me % 4 + 1) % NX, t, (me // 4) % 2), me // 8)
    w_from = (8 * t + 4 * c + (x + 3) % 4, z)

    barrier = pltpu.get_barrier_semaphore()
    peers = [zp(k) for k in range(1, NZ)] + [xp(k) for k in range(1, NX)] + [yp(k) for k in range(1, NY)]
    peers += [other, w_to, w_from]
    for dev in peers:
        pl.semaphore_signal(barrier, inc=1, device_id=dev, device_id_type=MESH)
    loads[0].wait()
    loads[1].wait()
    loads[2].wait()
    loads[3].wait()
    pl.semaphore_wait(barrier, len(peers))

    sent = []

    def go(copy):
        copy.start()
        sent.append(copy)

    def gather(buf, s, r, ring):
        def copy(n, src, dst, dev):
            return remote(src, dst, s.at[n], r.at[n], dev)

        def over_z(i):
            k = Z_RANKS[i]
            if not ring:
                return copy(i, buf.at[c, x, 0], buf.at[c, x, i], zp(k))
            way = 1 if k <= 4 else -1
            return copy(i, buf.at[c, x, Z_RANKS.index((k - way) % NZ)], buf.at[c, x, i], zp(way % NZ))

        def part(xx, group):
            first, count = Z_GROUPS[group]
            return buf.at[c, xx, pl.ds(first, count)]

        def near(group, way, came=False):
            ref = part((x - way + NX) % NX if came else x, group)
            return copy(8 + 2 * group + (way < 0), ref, ref, xp(way % NX))

        def far(group, came=False):
            way = 1 if group in GO_RIGHT else -1
            ref = part((x - 2 + NX) % NX if came else (x - way + NX) % NX, group)
            return copy(18 + group, ref, ref, xp(way % NX))

        def cross(k, came=False):
            ref = buf.at[1 - c if came else c, (x - k + NX) % NX]
            return copy(23 + k, ref, ref, other)

        for i in (1, 2) if ring else range(NZ - 1, 0, -1):
            go(over_z(i))
        for way in (1, -1):
            go(near(0, way))
        yield
        for group in range(1, 5):
            first, count = Z_GROUPS[group]
            for i in range(first, first + count):
                over_z(i).wait_recv()
                if ring and i + 2 < NZ:
                    go(over_z(i + 2))
            for way in (1, -1):
                go(near(group, way))
            for way in (1, -1):
                near(group - 1, way, True).wait_recv()
            go(far(group - 1))
            yield
        go(cross(0))
        for way in (1, -1):
            near(4, way, True).wait_recv()
        go(far(4))
        go(cross(1))
        go(cross(3))
        yield
        for group in range(5):
            far(group, True).wait_recv()
        go(cross(2))
        yield
        for k in range(NX):
            cross(k, True).wait_recv()
        yield

    wt_c, wt_z, wt_x = (me // 4) % 2, t, (me % 4 + 1) % NX

    def gather_weights():
        def copy(n, src, dst, dev):
            return remote(src, dst, wg_s.at[n], wg_r.at[n], dev)

        def over_x(k, came=False):
            ref = wbuf.at[c, 0, (x - k + NX) % NX if came else x]
            return copy(k, ref, ref, xp(k))

        def hop(i, way):
            before = Z_RANKS.index((Z_RANKS[i] - way) % NZ)
            if i < NZ - 1:
                return copy(4 + i, wbuf.at[c, before], wbuf.at[c, i], zp(way % NZ))
            part = pl.ds(0 if way == 1 else 2, 2)
            return copy(11 + (way == 1), wbuf.at[c, before, part], wbuf.at[c, i, part], zp(way % NZ))

        def cross(i, came=False):
            ref = wbuf.at[1 - c if came else c, i]
            return copy(13 + i, ref, ref, other)

        go(remote(wst, wbuf.at[wt_c, 0, wt_x], w0_s, w0_r, w_to))
        yield
        remote(wst, wbuf.at[c, 0, x], w0_s, w0_r, w_to).wait_recv()
        for k in (2, 1, 3):
            go(over_x(k))
        yield
        for k in (1, 3, 2):
            over_x(k, True).wait_recv()
        go(hop(1, 1))
        go(hop(2, -1))
        go(cross(0))
        yield
        for i, way in ((1, 1), (2, -1), (3, 1), (4, -1), (5, 1), (6, -1)):
            hop(i, way).wait_recv()
            go(hop(min(i + 2, NZ - 1), way))
            go(cross(i))
            if way == -1:
                yield
        for way in (1, -1):
            hop(NZ - 1, way).wait_recv()
        go(cross(NZ - 1))
        yield
        for i in range(NZ):
            cross(i, True).wait_recv()
        yield

    prompts = gather(kv, kv_s, kv_r, True)
    weights = gather_weights()

    next(prompts)
    next(weights, None)

    for copy in loads[4:]:
        copy.wait()

    lane = lax.broadcasted_iota(jnp.int32, (1, HD), 1)
    rows = []
    for base in (me, at(x, z, 1 - c)):
        found = jnp.full((1, HD), SLOTS, jnp.int32)
        for s in range(SLOTS):
            found = jnp.where(lane == prompt_ref[base * SLOTS + s], s, found)
        rows.append(found)
    table[0:1, :] = rows[0]
    table[1:2, :] = rows[1]
    table_copy = pltpu.make_async_copy(table, table_s, table_sem)
    table_copy.start()
    own[SLOTS] = jnp.zeros((2 * LP, HD), BF)
    sib[SLOTS] = jnp.zeros((2 * LP, HD), BF)

    lse_t[...] = spread_rows(lse[...])
    delta_t[...] = spread_rows(delta[...])

    next(prompts)
    next(prompts)
    next(prompts)
    next(weights, None)
    next(prompts)
    next(prompts)
    next(prompts)
    next(weights, None)
    next(prompts)

    key_row = lax.broadcasted_iota(jnp.int32, (2 * LP + 16, HD), 0)
    column = lax.broadcasted_iota(jnp.int32, (2 * LP + 16, HD), 1)
    col_r, col_t = (column // LR) % 2, column % LR
    in_own = key_row >= 2 * LP
    row_r = jnp.where(in_own, (key_row - 2 * LP) // LR, key_row // LP)
    seen = (row_r == col_r) & (jnp.logical_not(in_own) | ((key_row % LR) <= col_t))
    col_r1, col_t1 = col_r[0:1], col_t[0:1]

    def one_pair(pair):
        base = pl.multiple_of(pair * 16, 16)
        p0, p1 = prompt_ref[me * SLOTS + 2 * pair], prompt_ref[me * SLOTS + 2 * pair + 1]
        l0, l1 = len_ref[2 * pair], len_ref[2 * pair + 1]
        kv0, kv1 = (kv[p % 2, p // 16, rank((z - (p // 2) % 8 + NZ) % NZ)] for p in (p0, p1))
        keys = jnp.concatenate([kv0[:LP], kv1[:LP], rk[pl.ds(base, 16)]], axis=0)
        values = jnp.concatenate([kv0[LP:], kv1[LP:], rv[pl.ds(base, 16)]], axis=0)
        qp = jnp.concatenate([q[pl.ds(base, 16), h * HD : (h + 1) * HD] for h in range(HEADS)], axis=0)
        gp = jnp.concatenate([g[pl.ds(base, 16), h * HD : (h + 1) * HD] for h in range(HEADS)], axis=0)
        live = col_t1 < jnp.where(col_r1 == 0, l0, l1)
        scores = dot_nt(keys, qp) * SCALE
        probs = jnp.exp(scores - lse_t[pl.ds(pair, 1)])
        probs = jnp.where(seen & live, probs, 0.0)
        dprob = dot_nt(values, gp)
        dscore = (probs * (dprob - delta_t[pl.ds(pair, 1)])).astype(BF)
        dv = dot_nn(probs.astype(BF), gp)
        dk = dot_nn(dscore, qp)
        dq = dot_tn(dscore, keys) * SCALE
        for r in range(2):
            own[2 * pair + r, 0:LP] = dk[r * LP : (r + 1) * LP].astype(BF)
            own[2 * pair + r, LP : 2 * LP] = dv[r * LP : (r + 1) * LP].astype(BF)
        drk_ref[pl.ds(base, 16)] = (dk[2 * LP :] * SCALE).astype(BF)
        drv_ref[pl.ds(base, 16)] = dv[2 * LP :].astype(BF)
        for h in range(HEADS):
            dq_ref[pl.ds(base, 16), h * HD : (h + 1) * HD] = dq[h * 16 : (h + 1) * 16].astype(BF)

    def rc(i):
        return remote(own.at[pl.ds(4 * i, 4)], sib.at[pl.ds(4 * i, 4)], rc_s.at[i], rc_r.at[i], other)

    for i in range(4):
        one_pair(2 * i)
        one_pair(2 * i + 1)
        go(rc(i))
        for _ in range((0, 1, 0, 1)[i]):
            next(weights, None)

    table_copy.wait()
    for i in range(4):
        rc(i).wait_recv()

    def both_cores(j, part):
        rows = slice(LP * part, LP * (part + 1))
        return own[table_s[0, j], rows].astype(F32) + sib[table_s[1, j], rows].astype(F32)

    def rf(way, part):
        n = 0 if way == 1 else 1
        return remote(snd0.at[part, n], rcv0.at[part, n], rf_s.at[part, n], rf_r.at[part, n], xp(way % NX))

    def rn(way, part):
        n = 0 if way == 1 else 1
        return remote(snd1.at[part, n], rcv1.at[part, n], rn_s.at[part, n], rn_r.at[part, n], xp(way % NX))

    def rz(i, part):
        return remote(snd2.at[part, i], rcv2.at[part, i], rz_s.at[part, i], rz_r.at[part, i], zp(Z_RANKS[i]))

    def ry(k, part):
        rows = pl.ds(LP * part, LP)
        return remote(rcv3.at[0, rows], rcv3.at[k, rows], ry_s.at[part, k], ry_r.at[part, k], yp(k))

    def ahead(i):
        return (z + Z_RANKS[i]) % NZ

    for part in range(2):
        for way in (1, -1):
            first = 0 if way == 1 else 4
            for i in range(4):
                j = at((x + 2) % NX, ahead(first + i), c)
                snd0[part, first // 4, i] = both_cores(j, part).astype(BF)
            go(rf(way, part))
    for part in range(2):
        for way in (1, -1):
            n = 0 if way == 1 else 1
            for i in [i for i in range(NZ) if i // 4 != n] + [i for i in range(NZ) if i // 4 == n]:
                if i == 4 * n:
                    rf(way, part).wait_recv()
                total = both_cores(at((x + way) % NX, ahead(i), c), part)
                if i // 4 == n:
                    total = total + rcv0[part, n, i - 4 * n].astype(F32)
                snd1[part, n, i] = total.astype(BF)
            go(rn(way, part))
    next(weights, None)

    mine = [None, None]
    for part in range(2):
        for way in (1, -1):
            rn(way, part).wait_recv()
        for i in range(NZ - 1, -1, -1):
            total = both_cores(at(x, ahead(i), c), part)
            for n in range(2):
                total = total + rcv1[part, n, i].astype(F32)
            if i:
                snd2[part, i] = total.astype(BF)
                go(rz(i, part))
            else:
                mine[part] = total
    next(weights, None)
    for part in range(2):
        for i in range(1, NZ):
            rz(i, part).wait_recv()
            mine[part] = mine[part] + rcv2[part, i].astype(F32)
        rcv3[0, LP * part : LP * (part + 1)] = (mine[part] * SCALE if part == 0 else mine[part]).astype(BF)
        for k in Y_ORDER:
            go(ry(k, part))
    next(weights, None)

    def project(k):
        head = (t - k + NY) % NY
        place = rank((z - head + NZ) % NZ)
        grads = rcv3[k]
        both = jnp.concatenate([grads[:LP], grads[LP:]], axis=1)
        weights = []
        for cc in range(NC):
            for j in range(4):
                block = wbuf[cc, place, (j + 1) % NX]
                weights.append(jnp.concatenate([block[:WROWS], block[WROWS:]], axis=1))
        return dot_nt(both, jnp.concatenate(weights, axis=0))

    acc = project(0)
    for k in Y_NEAR:
        for part in range(2):
            ry(k, part).wait_recv()
        acc = acc + project(k)
    out_ref[...] = acc.astype(BF)

    for copy in sent:
        copy.wait_send()


def body(*args):
    vmem = pl.BlockSpec(memory_space=pltpu.VMEM)
    hbm = pl.BlockSpec(memory_space=pl.ANY)
    rows = SLOTS * LR
    dma = pltpu.SemaphoreType.DMA
    return pl.pallas_call(
        kernel,
        out_shape=(
            jax.ShapeDtypeStruct((rows, HEADS * HD), BF),
            jax.ShapeDtypeStruct((rows, HD), BF),
            jax.ShapeDtypeStruct((rows, HD), BF),
            jax.ShapeDtypeStruct((LP, 8 * WROWS), BF),
        ),
        in_specs=[hbm] * 12,
        out_specs=(vmem,) * 4,
        scratch_shapes=[
            pltpu.SMEM((64 * SLOTS,), jnp.int32),
            pltpu.SMEM((SLOTS,), jnp.int32),
            pltpu.VMEM((NC, NX, NZ, 2 * LP, HD), BF),
            pltpu.VMEM((2 * WROWS, HD), BF),
            pltpu.VMEM((NC, NZ, NX, 2 * WROWS, HD), BF),
            pltpu.VMEM((rows, HEADS * HD), BF),
            pltpu.VMEM((rows, HEADS * HD), BF),
            pltpu.VMEM((rows, HD), BF),
            pltpu.VMEM((rows, HD), BF),
            pltpu.VMEM((HEADS, rows), F32),
            pltpu.VMEM((HEADS, rows), F32),
            pltpu.VMEM((PAIRS, HD), F32),
            pltpu.VMEM((PAIRS, HD), F32),
            pltpu.VMEM((SLOTS + 1, 2 * LP, HD), BF),
            pltpu.VMEM((SLOTS + 1, 2 * LP, HD), BF),
            pltpu.VMEM((8, HD), jnp.int32),
            pltpu.SMEM((8, HD), jnp.int32),
            pltpu.VMEM((2, 2, NZ // 2, LP, HD), BF),
            pltpu.VMEM((2, 2, NZ // 2, LP, HD), BF),
            pltpu.VMEM((2, 2, NZ, LP, HD), BF),
            pltpu.VMEM((2, 2, NZ, LP, HD), BF),
            pltpu.VMEM((2, NZ, LP, HD), BF),
            pltpu.VMEM((2, NZ, LP, HD), BF),
            pltpu.VMEM((NY, 2 * LP, HD), BF),
            dma((12,)),
            dma,
            dma((27,)), dma((27,)), dma, dma, dma((27,)), dma((27,)),
            dma((4,)), dma((4,)), dma((2, 2)), dma((2, 2)), dma((2, 2)), dma((2, 2)),
            dma((2, NZ)), dma((2, NZ)), dma((2, NY)), dma((2, NY)),
        ],
        compiler_params=pltpu.CompilerParams(
            collective_id=0, has_side_effects=True, vmem_limit_bytes=62 << 20
        ),
        name="attention_back",
    )(*args)


def solution(mesh):
    split = P("dp", "tensor")
    return jax.shard_map(
        body,
        mesh=mesh,
        in_specs=(split,) * 8 + (P("tensor", "dp"),) * 2 + (P(), P("dp")),
        out_specs=(split,) * 4,
        check_vma=False,
    )
```

```python
import math

import jax
import jax.numpy as jnp
from jax import lax
from jax.experimental import pallas as pl
from jax.experimental.pallas import tpu as pltpu
from jax.sharding import PartitionSpec as P

HD = 128
HEADS = 8
LP = 64
LR = 8
SLOTS = 16
PAIRS = SLOTS // 2
NX, NZ, NC, NY = 4, 8, 2, 8
WROWS = 80
SCALE = 1.0 / math.sqrt(HD)
MESH = pl.DeviceIdType.MESH
BF, F32 = jnp.bfloat16, jnp.float32
Z_RANKS = (0, 1, 7, 2, 6, 3, 5, 4)
Z_GROUPS = ((0, 1), (1, 2), (3, 2), (5, 2), (7, 1))
GO_RIGHT = (0, 1, 4)
Y_ORDER = (4, 3, 5, 2, 6, 1, 7)
Y_NEAR = (1, 7, 2, 6, 3, 5, 4)


def dot_nt(a, b):
    return lax.dot_general(a, b, (((1,), (1,)), ((), ())), preferred_element_type=F32)


def dot_nn(a, b):
    return lax.dot_general(a, b, (((1,), (0,)), ((), ())), preferred_element_type=F32)


def dot_tn(a, b):
    return lax.dot_general(a, b, (((0,), (0,)), ((), ())), preferred_element_type=F32)


def rank(k):
    return jnp.where(k == 0, 0, jnp.where(k <= 4, 2 * k - 1, 16 - 2 * k))


def spread_rows(rows):
    lane = lax.broadcasted_iota(jnp.int32, (HEADS, HD), 1) // 16
    head = lax.broadcasted_iota(jnp.int32, (HEADS, HD), 0)
    turned = [rows if k == 0 else pltpu.roll(rows, 16 * k, 1) for k in range(8)]
    out = []
    for pair in range(PAIRS):
        picked = jnp.zeros((HEADS, HD), F32)
        for h in range(HEADS):
            picked = jnp.where((head == h) & (lane == h), turned[(h - pair) % 8], picked)
        out.append(jnp.sum(picked, axis=0, keepdims=True))
    return jnp.concatenate(out, axis=0)


def kernel(
    pk_ref, pv_ref, kw_ref, vw_ref, q_ref, rk_ref, rv_ref, g_ref, lse_ref, delta_ref, prompt_in, len_in,
    dq_out, drk_out, drv_out, input_out,
    dq_ref, drk_ref, drv_ref, out_ref, out_sem, prompt_ref, len_ref, kv, wst, wbuf, q, g, rk, rv, lse, delta, lse_t, delta_t,
    own, sib, table, table_s, snd0, rcv0, snd1, rcv1, snd2, rcv2, rcv3,
    load_sem, table_sem,
    kv_s, kv_r, w0_s, w0_r, wg_s, wg_r,
    rc_s, rc_r, rf_s, rf_r, rn_s, rn_r, rz_s, rz_r, ry_s, ry_r,
):
    me = lax.axis_index("dp")
    t = lax.axis_index("tensor")
    x, z, c = me // 16, (me // 2) % 8, me % 2

    def at(xx, zz, cc):
        return xx * 16 + zz * 2 + cc

    def xp(k):
        return (at((x + k) % NX, z, c), t)

    def zp(k):
        return (at(x, (z + k) % NZ, c), t)

    def yp(k):
        return (me, (t + k) % NY)

    other = (at(x, z, 1 - c), t)

    def remote(src, dst, s, r, dev):
        return pltpu.make_async_remote_copy(src_ref=src, dst_ref=dst, send_sem=s, recv_sem=r, device_id=dev, device_id_type=MESH)

    loads = [
        (pk_ref, kv.at[c, x, 0, 0:LP]),
        (pv_ref, kv.at[c, x, 0, LP : 2 * LP]),
        (kw_ref, wst.at[0:WROWS]),
        (vw_ref, wst.at[WROWS : 2 * WROWS]),
        (q_ref, q),
        (g_ref, g),
        (rk_ref, rk),
        (rv_ref, rv),
        (lse_ref, lse),
        (delta_ref, delta),
        (prompt_in, prompt_ref),
        (len_in, len_ref),
    ]
    loads = [pltpu.make_async_copy(a, b, load_sem.at[i]) for i, (a, b) in enumerate(loads)]
    for copy in loads:
        copy.start()

    w_to = (at((me % 4 + 1) % NX, t, (me // 4) % 2), me // 8)
    w_from = (8 * t + 4 * c + (x + 3) % 4, z)

    barrier = pltpu.get_barrier_semaphore()
    peers = [zp(k) for k in range(1, NZ)] + [xp(k) for k in range(1, NX)] + [yp(k) for k in range(1, NY)]
    peers += [other, w_to, w_from]
    for dev in peers:
        pl.semaphore_signal(barrier, inc=1, device_id=dev, device_id_type=MESH)
    loads[0].wait()
    loads[1].wait()
    loads[2].wait()
    loads[3].wait()
    pl.semaphore_wait(barrier, len(peers))

    sent = []

    def go(copy):
        copy.start()
        sent.append(copy)

    def gather(buf, s, r, ring):
        def copy(n, src, dst, dev):
            return remote(src, dst, s.at[n], r.at[n], dev)

        def over_z(i):
            k = Z_RANKS[i]
            if not ring:
                return copy(i, buf.at[c, x, 0], buf.at[c, x, i], zp(k))
            way = 1 if k <= 4 else -1
            return copy(i, buf.at[c, x, Z_RANKS.index((k - way) % NZ)], buf.at[c, x, i], zp(way % NZ))

        def part(xx, group):
            first, count = Z_GROUPS[group]
            return buf.at[c, xx, pl.ds(first, count)]

        def near(group, way, came=False):
            ref = part((x - way + NX) % NX if came else x, group)
            return copy(8 + 2 * group + (way < 0), ref, ref, xp(way % NX))

        def far(group, came=False):
            way = 1 if group in GO_RIGHT else -1
            ref = part((x - 2 + NX) % NX if came else (x - way + NX) % NX, group)
            return copy(18 + group, ref, ref, xp(way % NX))

        def cross(k, came=False):
            ref = buf.at[1 - c if came else c, (x - k + NX) % NX]
            return copy(23 + k, ref, ref, other)

        def cross_far(half, came=False):
            ref = buf.at[1 - c if came else c, (x - 2 + NX) % NX, pl.ds(5 * half, 5 - 2 * half)]
            return copy(25 if half else 27, ref, ref, other)

        for i in (1, 2) if ring else range(NZ - 1, 0, -1):
            go(over_z(i))
        for way in (1, -1):
            go(near(0, way))
        yield
        for group in range(1, 5):
            first, count = Z_GROUPS[group]
            for i in range(first, first + count):
                over_z(i).wait_recv()
                if ring and i + 2 < NZ:
                    go(over_z(i + 2))
            for way in (1, -1):
                go(near(group, way))
            for way in (1, -1):
                near(group - 1, way, True).wait_recv()
            go(far(group - 1))
            yield
        go(cross(0))
        for way in (1, -1):
            near(4, way, True).wait_recv()
        go(far(4))
        go(cross(1))
        go(cross(3))
        yield
        for half in range(2):
            for group in ((0, 1, 2), (3, 4))[half]:
                far(group, True).wait_recv()
            go(cross_far(half))
        yield
        for k in (0, 1, 3):
            cross(k, True).wait_recv()
        for half in range(2):
            cross_far(half, True).wait_recv()
        yield

    wt_c, wt_z, wt_x = (me // 4) % 2, t, (me % 4 + 1) % NX

    def gather_weights():
        def copy(n, src, dst, dev):
            return remote(src, dst, wg_s.at[n], wg_r.at[n], dev)

        def over_x(k, came=False):
            ref = wbuf.at[c, 0, (x - k + NX) % NX if came else x]
            return copy(k, ref, ref, xp(k))

        def hop(i, way):
            before = Z_RANKS.index((Z_RANKS[i] - way) % NZ)
            if i < NZ - 1:
                return copy(4 + i, wbuf.at[c, before], wbuf.at[c, i], zp(way % NZ))
            part = pl.ds(0 if way == 1 else 2, 2)
            return copy(11 + (way == 1), wbuf.at[c, before, part], wbuf.at[c, i, part], zp(way % NZ))

        def cross(i, came=False):
            ref = wbuf.at[1 - c if came else c, i]
            return copy(13 + i, ref, ref, other)

        go(remote(wst, wbuf.at[wt_c, 0, wt_x], w0_s, w0_r, w_to))
        yield
        remote(wst, wbuf.at[c, 0, x], w0_s, w0_r, w_to).wait_recv()
        for k in (2, 1, 3):
            go(over_x(k))
        yield
        for k in (1, 3, 2):
            over_x(k, True).wait_recv()
        go(hop(1, 1))
        go(hop(2, -1))
        go(cross(0))
        yield
        for i, way in ((1, 1), (2, -1), (3, 1), (4, -1), (5, 1), (6, -1)):
            hop(i, way).wait_recv()
            go(hop(min(i + 2, NZ - 1), way))
            go(cross(i))
            if way == -1:
                yield
        for way in (1, -1):
            hop(NZ - 1, way).wait_recv()
        go(cross(NZ - 1))
        yield
        for i in range(NZ):
            cross(i, True).wait_recv()
        yield

    prompts = gather(kv, kv_s, kv_r, True)
    weights = gather_weights()

    next(prompts)
    next(weights, None)

    next(prompts)
    next(prompts)
    next(weights, None)
    next(prompts)
    next(prompts)
    next(prompts)
    next(weights, None)
    next(prompts)
    for copy in loads[4:]:
        copy.wait()

    lane = lax.broadcasted_iota(jnp.int32, (1, HD), 1)
    rows = []
    for base in (me, at(x, z, 1 - c)):
        found = jnp.full((1, HD), SLOTS, jnp.int32)
        for s in range(SLOTS):
            found = jnp.where(lane == prompt_ref[base * SLOTS + s], s, found)
        rows.append(found)
    table[0:1, :] = rows[0]
    table[1:2, :] = rows[1]
    table_copy = pltpu.make_async_copy(table, table_s, table_sem)
    table_copy.start()
    own[SLOTS] = jnp.zeros((2 * LP, HD), BF)
    sib[SLOTS] = jnp.zeros((2 * LP, HD), BF)

    lse_t[...] = spread_rows(lse[...])
    delta_t[...] = spread_rows(delta[...])

    next(prompts)
    next(weights, None)

    key_row = lax.broadcasted_iota(jnp.int32, (2 * LP + 16, HD), 0)
    column = lax.broadcasted_iota(jnp.int32, (2 * LP + 16, HD), 1)
    col_r, col_t = (column // LR) % 2, column % LR
    in_own = key_row >= 2 * LP
    row_r = jnp.where(in_own, (key_row - 2 * LP) // LR, key_row // LP)
    seen = (row_r == col_r) & (jnp.logical_not(in_own) | ((key_row % LR) <= col_t))
    col_r1, col_t1 = col_r[0:1], col_t[0:1]

    def one_pair(pair):
        base = pl.multiple_of(pair * 16, 16)
        p0, p1 = prompt_ref[me * SLOTS + 2 * pair], prompt_ref[me * SLOTS + 2 * pair + 1]
        l0, l1 = len_ref[2 * pair], len_ref[2 * pair + 1]
        kv0, kv1 = (kv[p % 2, p // 16, rank((z - (p // 2) % 8 + NZ) % NZ)] for p in (p0, p1))
        keys = jnp.concatenate([kv0[:LP], kv1[:LP], rk[pl.ds(base, 16)]], axis=0)
        values = jnp.concatenate([kv0[LP:], kv1[LP:], rv[pl.ds(base, 16)]], axis=0)
        qp = jnp.concatenate([q[pl.ds(base, 16), h * HD : (h + 1) * HD] for h in range(HEADS)], axis=0)
        gp = jnp.concatenate([g[pl.ds(base, 16), h * HD : (h + 1) * HD] for h in range(HEADS)], axis=0)
        live = col_t1 < jnp.where(col_r1 == 0, l0, l1)
        scores = dot_nt(keys, qp) * SCALE
        probs = jnp.exp(scores - lse_t[pl.ds(pair, 1)])
        probs = jnp.where(seen & live, probs, 0.0)
        dprob = dot_nt(values, gp)
        dscore = (probs * (dprob - delta_t[pl.ds(pair, 1)])).astype(BF)
        dv = dot_nn(probs.astype(BF), gp)
        dk = dot_nn(dscore, qp)
        dq = dot_tn(dscore, keys) * SCALE
        for r in range(2):
            own[2 * pair + r, 0:LP] = dk[r * LP : (r + 1) * LP].astype(BF)
            own[2 * pair + r, LP : 2 * LP] = dv[r * LP : (r + 1) * LP].astype(BF)
        drk_ref[pl.ds(base, 16)] = (dk[2 * LP :] * SCALE).astype(BF)
        drv_ref[pl.ds(base, 16)] = dv[2 * LP :].astype(BF)
        for h in range(HEADS):
            dq_ref[pl.ds(base, 16), h * HD : (h + 1) * HD] = dq[h * 16 : (h + 1) * 16].astype(BF)

    def rc(i):
        return remote(own.at[pl.ds(4 * i, 4)], sib.at[pl.ds(4 * i, 4)], rc_s.at[i], rc_r.at[i], other)

    for i in range(4):
        one_pair(2 * i)
        one_pair(2 * i + 1)
        go(rc(i))
        for _ in range((0, 0, 0, 1)[i]):
            next(weights, None)

    stores = [
        pltpu.make_async_copy(a, b, out_sem.at[i])
        for i, (a, b) in enumerate(
            ((dq_ref, dq_out), (drk_ref, drk_out), (drv_ref, drv_out), (out_ref, input_out))
        )
    ]
    for copy in stores[:3]:
        copy.start()
    table_copy.wait()
    for i in range(4):
        rc(i).wait_recv()

    def both_cores(j, part):
        rows = slice(LP * part, LP * (part + 1))
        return own[table_s[0, j], rows].astype(F32) + sib[table_s[1, j], rows].astype(F32)

    def rf(way, part):
        n = 0 if way == 1 else 1
        return remote(snd0.at[part, n], rcv0.at[part, n], rf_s.at[part, n], rf_r.at[part, n], xp(way % NX))

    def rn(way, part):
        n = 0 if way == 1 else 1
        return remote(snd1.at[part, n], rcv1.at[part, n], rn_s.at[part, n], rn_r.at[part, n], xp(way % NX))

    def rz(i, part):
        return remote(snd2.at[part, i], rcv2.at[part, i], rz_s.at[part, i], rz_r.at[part, i], zp(Z_RANKS[i]))

    def ry(k, part):
        rows = pl.ds(LP * part, LP)
        return remote(rcv3.at[0, rows], rcv3.at[k, rows], ry_s.at[part, k], ry_r.at[part, k], yp(k))

    def ahead(i):
        return (z + Z_RANKS[i]) % NZ

    for part in range(2):
        for way in (1, -1):
            first = 0 if way == 1 else 4
            for i in range(4):
                j = at((x + 2) % NX, ahead(first + i), c)
                snd0[part, first // 4, i] = both_cores(j, part).astype(BF)
            go(rf(way, part))
    for part in range(2):
        for way in (1, -1):
            n = 0 if way == 1 else 1
            for i in [i for i in range(NZ) if i // 4 != n] + [i for i in range(NZ) if i // 4 == n]:
                if i == 4 * n:
                    rf(way, part).wait_recv()
                total = both_cores(at((x + way) % NX, ahead(i), c), part)
                if i // 4 == n:
                    total = total + rcv0[part, n, i - 4 * n].astype(F32)
                snd1[part, n, i] = total.astype(BF)
            go(rn(way, part))
    next(weights, None)

    mine = [None, None]
    for part in range(2):
        for way in (1, -1):
            rn(way, part).wait_recv()
        for i in range(NZ - 1, -1, -1):
            total = both_cores(at(x, ahead(i), c), part)
            for n in range(2):
                total = total + rcv1[part, n, i].astype(F32)
            if i:
                snd2[part, i] = total.astype(BF)
                go(rz(i, part))
            else:
                mine[part] = total
    next(weights, None)
    for part in range(2):
        for i in range(1, NZ):
            rz(i, part).wait_recv()
            mine[part] = mine[part] + rcv2[part, i].astype(F32)
        rcv3[0, LP * part : LP * (part + 1)] = (mine[part] * SCALE if part == 0 else mine[part]).astype(BF)
        for k in Y_ORDER:
            go(ry(k, part))
    next(weights, None)

    def project(k):
        head = (t - k + NY) % NY
        place = rank((z - head + NZ) % NZ)
        grads = rcv3[k]
        both = jnp.concatenate([grads[:LP], grads[LP:]], axis=1)
        weights = []
        for cc in range(NC):
            for j in range(4):
                block = wbuf[cc, place, (j + 1) % NX]
                weights.append(jnp.concatenate([block[:WROWS], block[WROWS:]], axis=1))
        return dot_nt(both, jnp.concatenate(weights, axis=0))

    acc = project(0)
    for k in Y_NEAR:
        for part in range(2):
            ry(k, part).wait_recv()
        acc = acc + project(k)
    out_ref[...] = acc.astype(BF)
    stores[3].start()
    for copy in sent:
        copy.wait_send()
    for copy in stores:
        copy.wait()


def store(*refs):
    arrays, outs, tiles, sem = refs[:4], refs[4:8], refs[8:12], refs[12]
    loads = [pltpu.make_async_copy(a, b, sem.at[0, i]) for i, (a, b) in enumerate(zip(arrays, tiles))]
    stores = [pltpu.make_async_copy(a, b, sem.at[1, i]) for i, (a, b) in enumerate(zip(tiles, outs))]
    for copy in loads:
        copy.start()
    for load, copy in zip(loads, stores):
        load.wait()
        copy.start()
    for copy in stores:
        copy.wait()


def body(*args):
    hbm = pl.BlockSpec(memory_space=pl.ANY)
    rows = SLOTS * LR
    dma = pltpu.SemaphoreType.DMA
    shapes = ((rows, HEADS * HD), (rows, HD), (rows, HD), (LP, 8 * WROWS))
    results = tuple(jax.ShapeDtypeStruct(shape, BF) for shape in shapes)
    grads = pl.pallas_call(
        kernel,
        out_shape=results,
        in_specs=[hbm] * 12,
        out_specs=(hbm,) * 4,
        scratch_shapes=[
            *(pltpu.VMEM(shape, BF) for shape in shapes),
            dma((4,)),
            pltpu.SMEM((64 * SLOTS,), jnp.int32),
            pltpu.SMEM((SLOTS,), jnp.int32),
            pltpu.VMEM((NC, NX, NZ, 2 * LP, HD), BF),
            pltpu.VMEM((2 * WROWS, HD), BF),
            pltpu.VMEM((NC, NZ, NX, 2 * WROWS, HD), BF),
            pltpu.VMEM((rows, HEADS * HD), BF),
            pltpu.VMEM((rows, HEADS * HD), BF),
            pltpu.VMEM((rows, HD), BF),
            pltpu.VMEM((rows, HD), BF),
            pltpu.VMEM((HEADS, rows), F32),
            pltpu.VMEM((HEADS, rows), F32),
            pltpu.VMEM((PAIRS, HD), F32),
            pltpu.VMEM((PAIRS, HD), F32),
            pltpu.VMEM((SLOTS + 1, 2 * LP, HD), BF),
            pltpu.VMEM((SLOTS + 1, 2 * LP, HD), BF),
            pltpu.VMEM((8, HD), jnp.int32),
            pltpu.SMEM((8, HD), jnp.int32),
            pltpu.VMEM((2, 2, NZ // 2, LP, HD), BF),
            pltpu.VMEM((2, 2, NZ // 2, LP, HD), BF),
            pltpu.VMEM((2, 2, NZ, LP, HD), BF),
            pltpu.VMEM((2, 2, NZ, LP, HD), BF),
            pltpu.VMEM((2, NZ, LP, HD), BF),
            pltpu.VMEM((2, NZ, LP, HD), BF),
            pltpu.VMEM((NY, 2 * LP, HD), BF),
            dma((12,)),
            dma,
            dma((28,)), dma((28,)), dma, dma, dma((28,)), dma((28,)),
            dma((4,)), dma((4,)), dma((2, 2)), dma((2, 2)), dma((2, 2)), dma((2, 2)),
            dma((2, NZ)), dma((2, NZ)), dma((2, NY)), dma((2, NY)),
        ],
        compiler_params=pltpu.CompilerParams(
            collective_id=0, has_side_effects=True, vmem_limit_bytes=62 << 20
        ),
        name="attention_back",
    )(*args)
    return pl.pallas_call(
        store,
        out_shape=results,
        in_specs=[hbm] * 4,
        out_specs=(hbm,) * 4,
        scratch_shapes=[*(pltpu.VMEM(shape, BF) for shape in shapes), dma((2, 4))],
        compiler_params=pltpu.CompilerParams(vmem_limit_bytes=62 << 20),
        name="store",
    )(*grads)


def solution(mesh):
    split = P("dp", "tensor")
    return jax.shard_map(
        body,
        mesh=mesh,
        in_specs=(split,) * 8 + (P("tensor", "dp"),) * 2 + (P(), P("dp")),
        out_specs=(split,) * 4,
        check_vma=False,
    )
```

```python
import math

import jax
import jax.numpy as jnp
from jax import lax
from jax.experimental import pallas as pl
from jax.experimental.pallas import tpu as pltpu
from jax.sharding import PartitionSpec as P

HD = 128
HEADS = 8
LP = 64
LR = 8
SLOTS = 16
PAIRS = SLOTS // 2
NX, NZ, NC, NY = 4, 8, 2, 8
WROWS = 80
PARTS = 4
PART = 2 * LP // PARTS
SCALE = 1.0 / math.sqrt(HD)
MESH = pl.DeviceIdType.MESH
BF, F32 = jnp.bfloat16, jnp.float32
Z_RANKS = (0, 1, 7, 2, 6, 3, 5, 4)
Z_GROUPS = ((0, 1), (1, 2), (3, 2), (5, 2), (7, 1))
GO_RIGHT = (0, 1, 4)
Y_ORDER = (4, 3, 5, 2, 6, 1, 7)
Y_NEAR = (1, 7, 2, 6, 3, 5, 4)


def dot_nt(a, b):
    return lax.dot_general(a, b, (((1,), (1,)), ((), ())), preferred_element_type=F32)


def dot_nn(a, b):
    return lax.dot_general(a, b, (((1,), (0,)), ((), ())), preferred_element_type=F32)


def dot_tn(a, b):
    return lax.dot_general(a, b, (((0,), (0,)), ((), ())), preferred_element_type=F32)


def rank(k):
    return jnp.where(k == 0, 0, jnp.where(k <= 4, 2 * k - 1, 16 - 2 * k))


def spread_rows(rows):
    lane = lax.broadcasted_iota(jnp.int32, (HEADS, HD), 1) // 16
    head = lax.broadcasted_iota(jnp.int32, (HEADS, HD), 0)
    turned = [rows if k == 0 else pltpu.roll(rows, 16 * k, 1) for k in range(8)]
    out = []
    for pair in range(PAIRS):
        picked = jnp.zeros((HEADS, HD), F32)
        for h in range(HEADS):
            picked = jnp.where((head == h) & (lane == h), turned[(h - pair) % 8], picked)
        out.append(jnp.sum(picked, axis=0, keepdims=True))
    return jnp.concatenate(out, axis=0)


def kernel(
    pk_ref, pv_ref, kw_ref, vw_ref, q_ref, rk_ref, rv_ref, g_ref, lse_ref, delta_ref, prompt_in, len_in,
    dq_out, drk_out, drv_out, input_out,
    dq_ref, drk_ref, drv_ref, out_ref, out_sem, prompt_ref, len_ref, kv, wst, wbuf, q, g, rk, rv, lse, delta, lse_t, delta_t,
    own, sib, table, table_s, snd0, rcv0, snd1, rcv1, snd2, rcv2, rcv3,
    load_sem, table_sem,
    kv_s, kv_r, w0_s, w0_r, wg_s, wg_r,
    rc_s, rc_r, rf_s, rf_r, rn_s, rn_r, rz_s, rz_r, ry_s, ry_r,
):
    me = lax.axis_index("dp")
    t = lax.axis_index("tensor")
    x, z, c = me // 16, (me // 2) % 8, me % 2

    def at(xx, zz, cc):
        return xx * 16 + zz * 2 + cc

    def xp(k):
        return (at((x + k) % NX, z, c), t)

    def zp(k):
        return (at(x, (z + k) % NZ, c), t)

    def yp(k):
        return (me, (t + k) % NY)

    other = (at(x, z, 1 - c), t)

    def remote(src, dst, s, r, dev):
        return pltpu.make_async_remote_copy(src_ref=src, dst_ref=dst, send_sem=s, recv_sem=r, device_id=dev, device_id_type=MESH)

    loads = [
        (pk_ref, kv.at[c, x, 0, 0:LP]),
        (pv_ref, kv.at[c, x, 0, LP : 2 * LP]),
        (kw_ref, wst.at[0:WROWS]),
        (vw_ref, wst.at[WROWS : 2 * WROWS]),
        (q_ref, q),
        (g_ref, g),
        (rk_ref, rk),
        (rv_ref, rv),
        (lse_ref, lse),
        (delta_ref, delta),
        (prompt_in, prompt_ref),
        (len_in, len_ref),
    ]
    loads = [pltpu.make_async_copy(a, b, load_sem.at[i]) for i, (a, b) in enumerate(loads)]
    for copy in loads:
        copy.start()

    w_to = (at((me % 4 + 1) % NX, t, (me // 4) % 2), me // 8)
    w_from = (8 * t + 4 * c + (x + 3) % 4, z)

    barrier = pltpu.get_barrier_semaphore()
    peers = [zp(k) for k in range(1, NZ)] + [xp(k) for k in range(1, NX)] + [yp(k) for k in range(1, NY)]
    peers += [other, w_to, w_from]
    for dev in peers:
        pl.semaphore_signal(barrier, inc=1, device_id=dev, device_id_type=MESH)
    loads[0].wait()
    loads[1].wait()
    loads[2].wait()
    loads[3].wait()
    pl.semaphore_wait(barrier, len(peers))

    sent = []

    def go(copy):
        copy.start()
        sent.append(copy)

    def gather(buf, s, r, ring):
        def copy(n, src, dst, dev):
            return remote(src, dst, s.at[n], r.at[n], dev)

        def over_z(i):
            k = Z_RANKS[i]
            if not ring:
                return copy(i, buf.at[c, x, 0], buf.at[c, x, i], zp(k))
            way = 1 if k <= 4 else -1
            return copy(i, buf.at[c, x, Z_RANKS.index((k - way) % NZ)], buf.at[c, x, i], zp(way % NZ))

        def part(xx, group):
            first, count = Z_GROUPS[group]
            return buf.at[c, xx, pl.ds(first, count)]

        def near(group, way, came=False):
            ref = part((x - way + NX) % NX if came else x, group)
            return copy(8 + 2 * group + (way < 0), ref, ref, xp(way % NX))

        def far(group, came=False):
            way = 1 if group in GO_RIGHT else -1
            ref = part((x - 2 + NX) % NX if came else (x - way + NX) % NX, group)
            return copy(18 + group, ref, ref, xp(way % NX))

        def cross(k, came=False):
            ref = buf.at[1 - c if came else c, (x - k + NX) % NX]
            return copy(23 + k, ref, ref, other)

        def cross_far(half, came=False):
            ref = buf.at[1 - c if came else c, (x - 2 + NX) % NX, pl.ds(5 * half, 5 - 2 * half)]
            return copy(25 if half else 27, ref, ref, other)

        for i in (1, 2) if ring else range(NZ - 1, 0, -1):
            go(over_z(i))
        for way in (1, -1):
            go(near(0, way))
        yield
        for group in range(1, 5):
            first, count = Z_GROUPS[group]
            for i in range(first, first + count):
                over_z(i).wait_recv()
                if ring and i + 2 < NZ:
                    go(over_z(i + 2))
            for way in (1, -1):
                go(near(group, way))
            for way in (1, -1):
                near(group - 1, way, True).wait_recv()
            go(far(group - 1))
            yield
        go(cross(0))
        for way in (1, -1):
            near(4, way, True).wait_recv()
        go(far(4))
        go(cross(1))
        go(cross(3))
        yield
        for half in range(2):
            for group in ((0, 1, 2), (3, 4))[half]:
                far(group, True).wait_recv()
            go(cross_far(half))
        yield
        for k in (0, 1, 3):
            cross(k, True).wait_recv()
        for half in range(2):
            cross_far(half, True).wait_recv()
        yield

    wt_c, wt_z, wt_x = (me // 4) % 2, t, (me % 4 + 1) % NX

    def gather_weights():
        def copy(n, src, dst, dev):
            return remote(src, dst, wg_s.at[n], wg_r.at[n], dev)

        def over_x(k, came=False):
            ref = wbuf.at[c, 0, (x - k + NX) % NX if came else x]
            return copy(k, ref, ref, xp(k))

        def hop(i, way):
            before = Z_RANKS.index((Z_RANKS[i] - way) % NZ)
            if i < NZ - 1:
                return copy(4 + i, wbuf.at[c, before], wbuf.at[c, i], zp(way % NZ))
            part = pl.ds(0 if way == 1 else 2, 2)
            return copy(11 + (way == 1), wbuf.at[c, before, part], wbuf.at[c, i, part], zp(way % NZ))

        def cross(i, came=False):
            ref = wbuf.at[1 - c if came else c, i]
            return copy(13 + i, ref, ref, other)

        go(remote(wst, wbuf.at[wt_c, 0, wt_x], w0_s, w0_r, w_to))
        yield
        remote(wst, wbuf.at[c, 0, x], w0_s, w0_r, w_to).wait_recv()
        for k in (2, 1, 3):
            go(over_x(k))
        yield
        for k in (1, 3, 2):
            over_x(k, True).wait_recv()
        go(hop(1, 1))
        go(hop(2, -1))
        go(cross(0))
        yield
        for i, way in ((1, 1), (2, -1), (3, 1), (4, -1), (5, 1), (6, -1)):
            hop(i, way).wait_recv()
            go(hop(min(i + 2, NZ - 1), way))
            go(cross(i))
            if way == -1:
                yield
        for way in (1, -1):
            hop(NZ - 1, way).wait_recv()
        go(cross(NZ - 1))
        yield
        for i in range(NZ):
            cross(i, True).wait_recv()
        yield

    prompts = gather(kv, kv_s, kv_r, True)
    weights = gather_weights()

    next(prompts)
    next(weights, None)

    next(prompts)
    next(weights, None)
    next(prompts)
    next(prompts)
    next(weights, None)
    next(prompts)
    next(prompts)
    next(prompts)
    next(weights, None)
    for copy in loads[4:]:
        copy.wait()

    lane = lax.broadcasted_iota(jnp.int32, (1, HD), 1)
    rows = []
    for base in (me, at(x, z, 1 - c)):
        found = jnp.full((1, HD), SLOTS, jnp.int32)
        for s in range(SLOTS):
            found = jnp.where(lane == prompt_ref[base * SLOTS + s], s, found)
        rows.append(found)
    table[0:1, :] = rows[0]
    table[1:2, :] = rows[1]
    table_copy = pltpu.make_async_copy(table, table_s, table_sem)
    table_copy.start()
    own[SLOTS] = jnp.zeros((2 * LP, HD), BF)
    sib[SLOTS] = jnp.zeros((2 * LP, HD), BF)

    lse_t[...] = spread_rows(lse[...])
    delta_t[...] = spread_rows(delta[...])

    next(prompts)

    key_row = lax.broadcasted_iota(jnp.int32, (2 * LP + 16, HD), 0)
    column = lax.broadcasted_iota(jnp.int32, (2 * LP + 16, HD), 1)
    col_r, col_t = (column // LR) % 2, column % LR
    in_own = key_row >= 2 * LP
    row_r = jnp.where(in_own, (key_row - 2 * LP) // LR, key_row // LP)
    seen = (row_r == col_r) & (jnp.logical_not(in_own) | ((key_row % LR) <= col_t))
    col_r1, col_t1 = col_r[0:1], col_t[0:1]

    def one_pair(pair):
        base = pl.multiple_of(pair * 16, 16)
        p0, p1 = prompt_ref[me * SLOTS + 2 * pair], prompt_ref[me * SLOTS + 2 * pair + 1]
        l0, l1 = len_ref[2 * pair], len_ref[2 * pair + 1]
        kv0, kv1 = (kv[p % 2, p // 16, rank((z - (p // 2) % 8 + NZ) % NZ)] for p in (p0, p1))
        keys = jnp.concatenate([kv0[:LP], kv1[:LP], rk[pl.ds(base, 16)]], axis=0)
        values = jnp.concatenate([kv0[LP:], kv1[LP:], rv[pl.ds(base, 16)]], axis=0)
        qp = jnp.concatenate([q[pl.ds(base, 16), h * HD : (h + 1) * HD] for h in range(HEADS)], axis=0)
        gp = jnp.concatenate([g[pl.ds(base, 16), h * HD : (h + 1) * HD] for h in range(HEADS)], axis=0)
        live = col_t1 < jnp.where(col_r1 == 0, l0, l1)
        scores = dot_nt(keys, qp) * SCALE
        probs = jnp.exp(scores - lse_t[pl.ds(pair, 1)])
        probs = jnp.where(seen & live, probs, 0.0)
        dprob = dot_nt(values, gp)
        dscore = (probs * (dprob - delta_t[pl.ds(pair, 1)])).astype(BF)
        dv = dot_nn(probs.astype(BF), gp)
        dk = dot_nn(dscore, qp)
        dq = dot_tn(dscore, keys) * SCALE
        for r in range(2):
            own[2 * pair + r, 0:LP] = dk[r * LP : (r + 1) * LP].astype(BF)
            own[2 * pair + r, LP : 2 * LP] = dv[r * LP : (r + 1) * LP].astype(BF)
        drk_ref[pl.ds(base, 16)] = (dk[2 * LP :] * SCALE).astype(BF)
        drv_ref[pl.ds(base, 16)] = dv[2 * LP :].astype(BF)
        for h in range(HEADS):
            dq_ref[pl.ds(base, 16), h * HD : (h + 1) * HD] = dq[h * 16 : (h + 1) * 16].astype(BF)

    def rc(i):
        return remote(own.at[pl.ds(4 * i, 4)], sib.at[pl.ds(4 * i, 4)], rc_s.at[i], rc_r.at[i], other)

    for i in range(4):
        one_pair(2 * i)
        one_pair(2 * i + 1)
        go(rc(i))
        for _ in range((0, 0, 0, 1)[i]):
            next(weights, None)

    stores = [
        pltpu.make_async_copy(a, b, out_sem.at[i])
        for i, (a, b) in enumerate(
            ((dq_ref, dq_out), (drk_ref, drk_out), (drv_ref, drv_out), (out_ref, input_out))
        )
    ]
    for copy in stores[:3]:
        copy.start()
    table_copy.wait()
    for i in range(4):
        rc(i).wait_recv()

    def both_cores(j, part):
        rows = slice(PART * part, PART * (part + 1))
        return own[table_s[0, j], rows].astype(F32) + sib[table_s[1, j], rows].astype(F32)

    def rf(way, part):
        n = 0 if way == 1 else 1
        return remote(snd0.at[part, n], rcv0.at[part, n], rf_s.at[part, n], rf_r.at[part, n], xp(way % NX))

    def rn(way, part):
        n = 0 if way == 1 else 1
        return remote(snd1.at[part, n], rcv1.at[part, n], rn_s.at[part, n], rn_r.at[part, n], xp(way % NX))

    def rz(i, part):
        return remote(snd2.at[part, i], rcv2.at[part, i], rz_s.at[part, i], rz_r.at[part, i], zp(Z_RANKS[i]))

    def ry(k, part):
        rows = pl.ds(PART * part, PART)
        return remote(rcv3.at[0, rows], rcv3.at[k, rows], ry_s.at[part, k], ry_r.at[part, k], yp(k))

    def ahead(i):
        return (z + Z_RANKS[i]) % NZ

    for part in range(PARTS):
        for way in (1, -1):
            first = 0 if way == 1 else 4
            for i in range(4):
                j = at((x + 2) % NX, ahead(first + i), c)
                snd0[part, first // 4, i] = both_cores(j, part).astype(BF)
            go(rf(way, part))
    for part in range(PARTS):
        for way in (1, -1):
            n = 0 if way == 1 else 1
            for i in [i for i in range(NZ) if i // 4 != n] + [i for i in range(NZ) if i // 4 == n]:
                if i == 4 * n:
                    rf(way, part).wait_recv()
                total = both_cores(at((x + way) % NX, ahead(i), c), part)
                if i // 4 == n:
                    total = total + rcv0[part, n, i - 4 * n].astype(F32)
                snd1[part, n, i] = total.astype(BF)
            go(rn(way, part))
    next(weights, None)

    mine = [None] * PARTS
    for part in range(PARTS):
        for way in (1, -1):
            rn(way, part).wait_recv()
        for i in range(NZ - 1, -1, -1):
            total = both_cores(at(x, ahead(i), c), part)
            for n in range(2):
                total = total + rcv1[part, n, i].astype(F32)
            if i:
                snd2[part, i] = total.astype(BF)
                go(rz(i, part))
            else:
                mine[part] = total
    next(weights, None)
    for part in range(PARTS):
        for i in range(1, NZ):
            rz(i, part).wait_recv()
            mine[part] = mine[part] + rcv2[part, i].astype(F32)
        rcv3[0, PART * part : PART * (part + 1)] = (mine[part] * SCALE if PART * part < LP else mine[part]).astype(BF)
        for k in Y_ORDER:
            go(ry(k, part))
    next(weights, None)

    def project(k):
        head = (t - k + NY) % NY
        place = rank((z - head + NZ) % NZ)
        grads = rcv3[k]
        both = jnp.concatenate([grads[:LP], grads[LP:]], axis=1)
        weights = []
        for cc in range(NC):
            for j in range(4):
                block = wbuf[cc, place, (j + 1) % NX]
                weights.append(jnp.concatenate([block[:WROWS], block[WROWS:]], axis=1))
        return dot_nt(both, jnp.concatenate(weights, axis=0))

    acc = project(0)
    for k in Y_NEAR:
        for part in range(PARTS):
            ry(k, part).wait_recv()
        acc = acc + project(k)
    out_ref[...] = acc.astype(BF)
    stores[3].start()
    for copy in sent:
        copy.wait_send()
    for copy in stores:
        copy.wait()


def store(*refs):
    arrays, outs, tiles, sem = refs[:4], refs[4:8], refs[8:12], refs[12]
    loads = [pltpu.make_async_copy(a, b, sem.at[0, i]) for i, (a, b) in enumerate(zip(arrays, tiles))]
    stores = [pltpu.make_async_copy(a, b, sem.at[1, i]) for i, (a, b) in enumerate(zip(tiles, outs))]
    for copy in loads:
        copy.start()
    for load, copy in zip(loads, stores):
        load.wait()
        copy.start()
    for copy in stores:
        copy.wait()


def body(*args):
    hbm = pl.BlockSpec(memory_space=pl.ANY)
    rows = SLOTS * LR
    dma = pltpu.SemaphoreType.DMA
    shapes = ((rows, HEADS * HD), (rows, HD), (rows, HD), (LP, 8 * WROWS))
    results = tuple(jax.ShapeDtypeStruct(shape, BF) for shape in shapes)
    grads = pl.pallas_call(
        kernel,
        out_shape=results,
        in_specs=[hbm] * 12,
        out_specs=(hbm,) * 4,
        scratch_shapes=[
            *(pltpu.VMEM(shape, BF) for shape in shapes),
            dma((4,)),
            pltpu.SMEM((64 * SLOTS,), jnp.int32),
            pltpu.SMEM((SLOTS,), jnp.int32),
            pltpu.VMEM((NC, NX, NZ, 2 * LP, HD), BF),
            pltpu.VMEM((2 * WROWS, HD), BF),
            pltpu.VMEM((NC, NZ, NX, 2 * WROWS, HD), BF),
            pltpu.VMEM((rows, HEADS * HD), BF),
            pltpu.VMEM((rows, HEADS * HD), BF),
            pltpu.VMEM((rows, HD), BF),
            pltpu.VMEM((rows, HD), BF),
            pltpu.VMEM((HEADS, rows), F32),
            pltpu.VMEM((HEADS, rows), F32),
            pltpu.VMEM((PAIRS, HD), F32),
            pltpu.VMEM((PAIRS, HD), F32),
            pltpu.VMEM((SLOTS + 1, 2 * LP, HD), BF),
            pltpu.VMEM((SLOTS + 1, 2 * LP, HD), BF),
            pltpu.VMEM((8, HD), jnp.int32),
            pltpu.SMEM((8, HD), jnp.int32),
            pltpu.VMEM((PARTS, 2, NZ // 2, PART, HD), BF),
            pltpu.VMEM((PARTS, 2, NZ // 2, PART, HD), BF),
            pltpu.VMEM((PARTS, 2, NZ, PART, HD), BF),
            pltpu.VMEM((PARTS, 2, NZ, PART, HD), BF),
            pltpu.VMEM((PARTS, NZ, PART, HD), BF),
            pltpu.VMEM((PARTS, NZ, PART, HD), BF),
            pltpu.VMEM((NY, 2 * LP, HD), BF),
            dma((12,)),
            dma,
            dma((28,)), dma((28,)), dma, dma, dma((28,)), dma((28,)),
            dma((4,)), dma((4,)), dma((PARTS, 2)), dma((PARTS, 2)), dma((PARTS, 2)), dma((PARTS, 2)),
            dma((PARTS, NZ)), dma((PARTS, NZ)), dma((PARTS, NY)), dma((PARTS, NY)),
        ],
        compiler_params=pltpu.CompilerParams(
            collective_id=0, has_side_effects=True, vmem_limit_bytes=62 << 20
        ),
        name="attention_back",
    )(*args)
    return pl.pallas_call(
        store,
        out_shape=results,
        in_specs=[hbm] * 4,
        out_specs=(hbm,) * 4,
        scratch_shapes=[*(pltpu.VMEM(shape, BF) for shape in shapes), dma((2, 4))],
        compiler_params=pltpu.CompilerParams(vmem_limit_bytes=62 << 20),
        name="store",
    )(*grads)


def solution(mesh):
    split = P("dp", "tensor")
    return jax.shard_map(
        body,
        mesh=mesh,
        in_specs=(split,) * 8 + (P("tensor", "dp"),) * 2 + (P(), P("dp")),
        out_specs=(split,) * 4,
        check_vma=False,
    )
```

```python
import math

import jax
import jax.numpy as jnp
from jax import lax
from jax.experimental import pallas as pl
from jax.experimental.pallas import tpu as pltpu
from jax.sharding import PartitionSpec as P

HD = 128
HEADS = 8
LP = 64
LR = 8
SLOTS = 16
PAIRS = SLOTS // 2
NX, NZ, NC, NY = 4, 8, 2, 8
WROWS = 80
PARTS = 4
PART = 2 * LP // PARTS
SCALE = 1.0 / math.sqrt(HD)
MESH = pl.DeviceIdType.MESH
BF, F32 = jnp.bfloat16, jnp.float32
Z_RANKS = (0, 1, 7, 2, 6, 3, 5, 4)
Z_GROUPS = ((0, 1), (1, 2), (3, 2), (5, 2), (7, 1))
GO_RIGHT = (0, 1, 4)
Y_ORDER = (4, 3, 5, 2, 6, 1, 7)
Y_NEAR = (1, 7, 2, 6, 3, 5, 4)


def dot_nt(a, b):
    return lax.dot_general(a, b, (((1,), (1,)), ((), ())), preferred_element_type=F32)


def dot_nn(a, b):
    return lax.dot_general(a, b, (((1,), (0,)), ((), ())), preferred_element_type=F32)


def dot_tn(a, b):
    return lax.dot_general(a, b, (((0,), (0,)), ((), ())), preferred_element_type=F32)


def rank(k):
    return jnp.where(k == 0, 0, jnp.where(k <= 4, 2 * k - 1, 16 - 2 * k))


def spread_rows(rows):
    lane = lax.broadcasted_iota(jnp.int32, (HEADS, HD), 1) // 16
    head = lax.broadcasted_iota(jnp.int32, (HEADS, HD), 0)
    turned = [rows if k == 0 else pltpu.roll(rows, 16 * k, 1) for k in range(8)]
    out = []
    for pair in range(PAIRS):
        picked = jnp.zeros((HEADS, HD), F32)
        for h in range(HEADS):
            picked = jnp.where((head == h) & (lane == h), turned[(h - pair) % 8], picked)
        out.append(jnp.sum(picked, axis=0, keepdims=True))
    return jnp.concatenate(out, axis=0)


def kernel(
    pk_ref, pv_ref, kw_ref, vw_ref, q_ref, rk_ref, rv_ref, g_ref, lse_ref, delta_ref, prompt_in, len_in,
    dq_out, drk_out, drv_out, input_out,
    dq_ref, drk_ref, drv_ref, out_ref, out_sem, prompt_ref, len_ref, kv, wst, wbuf, q, g, rk, rv, lse, delta, lse_t, delta_t,
    own, sib, table, table_s, snd0, rcv0, snd1, rcv1, snd2, rcv2, rcv3,
    load_sem, table_sem,
    kv_s, kv_r, w0_s, w0_r, wg_s, wg_r,
    rc_s, rc_r, rf_s, rf_r, rn_s, rn_r, rz_s, rz_r, ry_s, ry_r,
):
    me = lax.axis_index("dp")
    t = lax.axis_index("tensor")
    x, z, c = me // 16, (me // 2) % 8, me % 2

    def at(xx, zz, cc):
        return xx * 16 + zz * 2 + cc

    def xp(k):
        return (at((x + k) % NX, z, c), t)

    def zp(k):
        return (at(x, (z + k) % NZ, c), t)

    def yp(k):
        return (me, (t + k) % NY)

    other = (at(x, z, 1 - c), t)

    def remote(src, dst, s, r, dev):
        return pltpu.make_async_remote_copy(src_ref=src, dst_ref=dst, send_sem=s, recv_sem=r, device_id=dev, device_id_type=MESH)

    loads = [
        (pk_ref, kv.at[c, x, 0, 0:LP]),
        (pv_ref, kv.at[c, x, 0, LP : 2 * LP]),
        (kw_ref, wst.at[0:WROWS]),
        (vw_ref, wst.at[WROWS : 2 * WROWS]),
        (q_ref, q),
        (g_ref, g),
        (rk_ref, rk),
        (rv_ref, rv),
        (lse_ref, lse),
        (delta_ref, delta),
        (prompt_in, prompt_ref),
        (len_in, len_ref),
    ]
    loads = [pltpu.make_async_copy(a, b, load_sem.at[i]) for i, (a, b) in enumerate(loads)]
    for copy in loads:
        copy.start()

    w_to = (at((me % 4 + 1) % NX, t, (me // 4) % 2), me // 8)
    w_from = (8 * t + 4 * c + (x + 3) % 4, z)

    barrier = pltpu.get_barrier_semaphore()
    peers = [zp(k) for k in range(1, NZ)] + [xp(k) for k in range(1, NX)] + [yp(k) for k in range(1, NY)]
    peers += [other, w_to, w_from]
    for dev in peers:
        pl.semaphore_signal(barrier, inc=1, device_id=dev, device_id_type=MESH)
    loads[0].wait()
    loads[1].wait()
    loads[2].wait()
    loads[3].wait()
    pl.semaphore_wait(barrier, len(peers))

    sent = []

    def go(copy):
        copy.start()
        sent.append(copy)

    def gather(buf, s, r, ring):
        def copy(n, src, dst, dev):
            return remote(src, dst, s.at[n], r.at[n], dev)

        def over_z(i):
            k = Z_RANKS[i]
            if not ring:
                return copy(i, buf.at[c, x, 0], buf.at[c, x, i], zp(k))
            way = 1 if k <= 4 else -1
            return copy(i, buf.at[c, x, Z_RANKS.index((k - way) % NZ)], buf.at[c, x, i], zp(way % NZ))

        def part(xx, group):
            first, count = Z_GROUPS[group]
            return buf.at[c, xx, pl.ds(first, count)]

        def near(group, way, came=False):
            ref = part((x - way + NX) % NX if came else x, group)
            return copy(8 + 2 * group + (way < 0), ref, ref, xp(way % NX))

        def far(group, came=False):
            way = 1 if group in GO_RIGHT else -1
            ref = part((x - 2 + NX) % NX if came else (x - way + NX) % NX, group)
            return copy(18 + group, ref, ref, xp(way % NX))

        def cross(k, came=False):
            ref = buf.at[1 - c if came else c, (x - k + NX) % NX]
            return copy(23 + k, ref, ref, other)

        def cross_far(half, came=False):
            ref = buf.at[1 - c if came else c, (x - 2 + NX) % NX, pl.ds(5 * half, 5 - 2 * half)]
            return copy(25 if half else 27, ref, ref, other)

        for i in (1, 2) if ring else range(NZ - 1, 0, -1):
            go(over_z(i))
        for way in (1, -1):
            go(near(0, way))
        yield
        for group in range(1, 5):
            first, count = Z_GROUPS[group]
            for i in range(first, first + count):
                over_z(i).wait_recv()
                if ring and i + 2 < NZ:
                    go(over_z(i + 2))
            for way in (1, -1):
                go(near(group, way))
            for way in (1, -1):
                near(group - 1, way, True).wait_recv()
            go(far(group - 1))
            yield
        go(cross(0))
        for way in (1, -1):
            near(4, way, True).wait_recv()
        go(far(4))
        go(cross(1))
        go(cross(3))
        yield
        for half in range(2):
            for group in ((0, 1, 2), (3, 4))[half]:
                far(group, True).wait_recv()
            go(cross_far(half))
        yield
        for k in (0, 1, 3):
            cross(k, True).wait_recv()
        for half in range(2):
            cross_far(half, True).wait_recv()
        yield

    wt_c, wt_z, wt_x = (me // 4) % 2, t, (me % 4 + 1) % NX

    def gather_weights():
        def copy(n, src, dst, dev):
            return remote(src, dst, wg_s.at[n], wg_r.at[n], dev)

        def over_x(k, came=False):
            ref = wbuf.at[c, 0, (x - k + NX) % NX if came else x]
            return copy(k, ref, ref, xp(k))

        def hop(i, way):
            before = Z_RANKS.index((Z_RANKS[i] - way) % NZ)
            if i < NZ - 1:
                return copy(4 + i, wbuf.at[c, before], wbuf.at[c, i], zp(way % NZ))
            part = pl.ds(0 if way == 1 else 2, 2)
            return copy(11 + (way == 1), wbuf.at[c, before, part], wbuf.at[c, i, part], zp(way % NZ))

        def cross(i, came=False):
            ref = wbuf.at[1 - c if came else c, i]
            return copy(13 + i, ref, ref, other)

        go(remote(wst, wbuf.at[wt_c, 0, wt_x], w0_s, w0_r, w_to))
        yield
        remote(wst, wbuf.at[c, 0, x], w0_s, w0_r, w_to).wait_recv()
        for k in (2, 1, 3):
            go(over_x(k))
        yield
        for k in (1, 3, 2):
            over_x(k, True).wait_recv()
        go(hop(1, 1))
        go(hop(2, -1))
        go(cross(0))
        yield
        for i, way in ((1, 1), (2, -1), (3, 1), (4, -1), (5, 1), (6, -1)):
            hop(i, way).wait_recv()
            go(hop(min(i + 2, NZ - 1), way))
            go(cross(i))
            if way == -1:
                yield
        for way in (1, -1):
            hop(NZ - 1, way).wait_recv()
        go(cross(NZ - 1))
        yield
        for i in range(NZ):
            cross(i, True).wait_recv()
        yield

    prompts = gather(kv, kv_s, kv_r, True)
    weights = gather_weights()

    next(prompts)
    next(weights, None)

    next(prompts)
    next(weights, None)
    next(prompts)
    next(prompts)
    next(weights, None)
    next(prompts)
    next(prompts)
    next(prompts)
    next(weights, None)
    for copy in loads[4:]:
        copy.wait()

    lane = lax.broadcasted_iota(jnp.int32, (1, HD), 1)
    rows = []
    for base in (me, at(x, z, 1 - c)):
        found = jnp.full((1, HD), SLOTS, jnp.int32)
        for s in range(SLOTS):
            found = jnp.where(lane == prompt_ref[base * SLOTS + s], s, found)
        rows.append(found)
    table[0:1, :] = rows[0]
    table[1:2, :] = rows[1]
    table_copy = pltpu.make_async_copy(table, table_s, table_sem)
    table_copy.start()
    own[SLOTS] = jnp.zeros((2 * LP, HD), BF)
    sib[SLOTS] = jnp.zeros((2 * LP, HD), BF)

    lse_t[...] = spread_rows(lse[...])
    delta_t[...] = spread_rows(delta[...])

    next(prompts)

    key_row = lax.broadcasted_iota(jnp.int32, (2 * LP + 16, HD), 0)
    column = lax.broadcasted_iota(jnp.int32, (2 * LP + 16, HD), 1)
    col_r, col_t = (column // LR) % 2, column % LR
    in_own = key_row >= 2 * LP
    row_r = jnp.where(in_own, (key_row - 2 * LP) // LR, key_row // LP)
    seen = (row_r == col_r) & (jnp.logical_not(in_own) | ((key_row % LR) <= col_t))
    col_r1, col_t1 = col_r[0:1], col_t[0:1]

    def one_pair(pair):
        base = pl.multiple_of(pair * 16, 16)
        p0, p1 = prompt_ref[me * SLOTS + 2 * pair], prompt_ref[me * SLOTS + 2 * pair + 1]
        l0, l1 = len_ref[2 * pair], len_ref[2 * pair + 1]
        kv0, kv1 = (kv[p % 2, p // 16, rank((z - (p // 2) % 8 + NZ) % NZ)] for p in (p0, p1))
        keys = jnp.concatenate([kv0[:LP], kv1[:LP], rk[pl.ds(base, 16)]], axis=0)
        values = jnp.concatenate([kv0[LP:], kv1[LP:], rv[pl.ds(base, 16)]], axis=0)
        qp = jnp.concatenate([q[pl.ds(base, 16), h * HD : (h + 1) * HD] for h in range(HEADS)], axis=0)
        gp = jnp.concatenate([g[pl.ds(base, 16), h * HD : (h + 1) * HD] for h in range(HEADS)], axis=0)
        live = col_t1 < jnp.where(col_r1 == 0, l0, l1)
        scores = dot_nt(keys, qp) * SCALE
        probs = jnp.exp(scores - lse_t[pl.ds(pair, 1)])
        probs = jnp.where(seen & live, probs, 0.0)
        dprob = dot_nt(values, gp)
        dscore = (probs * (dprob - delta_t[pl.ds(pair, 1)])).astype(BF)
        dv = dot_nn(probs.astype(BF), gp)
        dk = dot_nn(dscore, qp)
        dq = dot_tn(dscore, keys) * SCALE
        for r in range(2):
            own[2 * pair + r, 0:LP] = dk[r * LP : (r + 1) * LP].astype(BF)
            own[2 * pair + r, LP : 2 * LP] = dv[r * LP : (r + 1) * LP].astype(BF)
        drk_ref[pl.ds(base, 16)] = (dk[2 * LP :] * SCALE).astype(BF)
        drv_ref[pl.ds(base, 16)] = dv[2 * LP :].astype(BF)
        for h in range(HEADS):
            dq_ref[pl.ds(base, 16), h * HD : (h + 1) * HD] = dq[h * 16 : (h + 1) * 16].astype(BF)

    def rc(i):
        return remote(own.at[pl.ds(4 * i, 4)], sib.at[pl.ds(4 * i, 4)], rc_s.at[i], rc_r.at[i], other)

    for i in range(4):
        one_pair(2 * i)
        one_pair(2 * i + 1)
        go(rc(i))

    stores = [
        pltpu.make_async_copy(a, b, out_sem.at[i])
        for i, (a, b) in enumerate(
            ((dq_ref, dq_out), (drk_ref, drk_out), (drv_ref, drv_out), (out_ref, input_out))
        )
    ]
    for copy in stores[:3]:
        copy.start()
    table_copy.wait()
    for i in range(4):
        rc(i).wait_recv()

    def both_cores(j, part):
        rows = slice(PART * part, PART * (part + 1))
        return own[table_s[0, j], rows].astype(F32) + sib[table_s[1, j], rows].astype(F32)

    def rf(way, part):
        n = 0 if way == 1 else 1
        return remote(snd0.at[part, n], rcv0.at[part, n], rf_s.at[part, n], rf_r.at[part, n], xp(way % NX))

    def rn(way, part):
        n = 0 if way == 1 else 1
        return remote(snd1.at[part, n], rcv1.at[part, n], rn_s.at[part, n], rn_r.at[part, n], xp(way % NX))

    def rz(i, part):
        return remote(snd2.at[part, i], rcv2.at[part, i], rz_s.at[part, i], rz_r.at[part, i], zp(Z_RANKS[i]))

    def ry(k, part):
        rows = pl.ds(PART * part, PART)
        return remote(rcv3.at[0, rows], rcv3.at[k, rows], ry_s.at[part, k], ry_r.at[part, k], yp(k))

    def ahead(i):
        return (z + Z_RANKS[i]) % NZ

    for part in range(PARTS):
        for way in (1, -1):
            first = 0 if way == 1 else 4
            for i in range(4):
                j = at((x + 2) % NX, ahead(first + i), c)
                snd0[part, first // 4, i] = both_cores(j, part).astype(BF)
            go(rf(way, part))
    next(weights, None)
    for part in range(PARTS):
        for way in (1, -1):
            n = 0 if way == 1 else 1
            for i in [i for i in range(NZ) if i // 4 != n] + [i for i in range(NZ) if i // 4 == n]:
                if i == 4 * n:
                    rf(way, part).wait_recv()
                total = both_cores(at((x + way) % NX, ahead(i), c), part)
                if i // 4 == n:
                    total = total + rcv0[part, n, i - 4 * n].astype(F32)
                snd1[part, n, i] = total.astype(BF)
            go(rn(way, part))
    next(weights, None)

    mine = [None] * PARTS
    for part in range(PARTS):
        for way in (1, -1):
            rn(way, part).wait_recv()
        for i in range(NZ - 1, -1, -1):
            total = both_cores(at(x, ahead(i), c), part)
            for n in range(2):
                total = total + rcv1[part, n, i].astype(F32)
            if i:
                snd2[part, i] = total.astype(BF)
                go(rz(i, part))
            else:
                mine[part] = total
    next(weights, None)
    for part in range(PARTS):
        for i in range(1, NZ):
            rz(i, part).wait_recv()
            mine[part] = mine[part] + rcv2[part, i].astype(F32)
        rcv3[0, PART * part : PART * (part + 1)] = (mine[part] * SCALE if PART * part < LP else mine[part]).astype(BF)
        for k in Y_ORDER:
            go(ry(k, part))
    next(weights, None)

    def project(k):
        head = (t - k + NY) % NY
        place = rank((z - head + NZ) % NZ)
        grads = rcv3[k]
        both = jnp.concatenate([grads[:LP], grads[LP:]], axis=1)
        weights = []
        for cc in range(NC):
            for j in range(4):
                block = wbuf[cc, place, (j + 1) % NX]
                weights.append(jnp.concatenate([block[:WROWS], block[WROWS:]], axis=1))
        return dot_nt(both, jnp.concatenate(weights, axis=0))

    acc = project(0)
    for k in Y_NEAR:
        for part in range(PARTS):
            ry(k, part).wait_recv()
        acc = acc + project(k)
    out_ref[...] = acc.astype(BF)
    stores[3].start()
    for copy in sent:
        copy.wait_send()
    for copy in stores:
        copy.wait()


def store(*refs):
    arrays, outs, tiles, sem = refs[:4], refs[4:8], refs[8:12], refs[12]
    loads = [pltpu.make_async_copy(a, b, sem.at[0, i]) for i, (a, b) in enumerate(zip(arrays, tiles))]
    stores = [pltpu.make_async_copy(a, b, sem.at[1, i]) for i, (a, b) in enumerate(zip(tiles, outs))]
    for copy in loads:
        copy.start()
    for load, copy in zip(loads, stores):
        load.wait()
        copy.start()
    for copy in stores:
        copy.wait()


def body(*args):
    hbm = pl.BlockSpec(memory_space=pl.ANY)
    rows = SLOTS * LR
    dma = pltpu.SemaphoreType.DMA
    shapes = ((rows, HEADS * HD), (rows, HD), (rows, HD), (LP, 8 * WROWS))
    results = tuple(jax.ShapeDtypeStruct(shape, BF) for shape in shapes)
    grads = pl.pallas_call(
        kernel,
        out_shape=results,
        in_specs=[hbm] * 12,
        out_specs=(hbm,) * 4,
        scratch_shapes=[
            *(pltpu.VMEM(shape, BF) for shape in shapes),
            dma((4,)),
            pltpu.SMEM((64 * SLOTS,), jnp.int32),
            pltpu.SMEM((SLOTS,), jnp.int32),
            pltpu.VMEM((NC, NX, NZ, 2 * LP, HD), BF),
            pltpu.VMEM((2 * WROWS, HD), BF),
            pltpu.VMEM((NC, NZ, NX, 2 * WROWS, HD), BF),
            pltpu.VMEM((rows, HEADS * HD), BF),
            pltpu.VMEM((rows, HEADS * HD), BF),
            pltpu.VMEM((rows, HD), BF),
            pltpu.VMEM((rows, HD), BF),
            pltpu.VMEM((HEADS, rows), F32),
            pltpu.VMEM((HEADS, rows), F32),
            pltpu.VMEM((PAIRS, HD), F32),
            pltpu.VMEM((PAIRS, HD), F32),
            pltpu.VMEM((SLOTS + 1, 2 * LP, HD), BF),
            pltpu.VMEM((SLOTS + 1, 2 * LP, HD), BF),
            pltpu.VMEM((8, HD), jnp.int32),
            pltpu.SMEM((8, HD), jnp.int32),
            pltpu.VMEM((PARTS, 2, NZ // 2, PART, HD), BF),
            pltpu.VMEM((PARTS, 2, NZ // 2, PART, HD), BF),
            pltpu.VMEM((PARTS, 2, NZ, PART, HD), BF),
            pltpu.VMEM((PARTS, 2, NZ, PART, HD), BF),
            pltpu.VMEM((PARTS, NZ, PART, HD), BF),
            pltpu.VMEM((PARTS, NZ, PART, HD), BF),
            pltpu.VMEM((NY, 2 * LP, HD), BF),
            dma((12,)),
            dma,
            dma((28,)), dma((28,)), dma, dma, dma((28,)), dma((28,)),
            dma((4,)), dma((4,)), dma((PARTS, 2)), dma((PARTS, 2)), dma((PARTS, 2)), dma((PARTS, 2)),
            dma((PARTS, NZ)), dma((PARTS, NZ)), dma((PARTS, NY)), dma((PARTS, NY)),
        ],
        compiler_params=pltpu.CompilerParams(
            collective_id=0, has_side_effects=True, vmem_limit_bytes=62 << 20
        ),
        name="attention_back",
    )(*args)
    return pl.pallas_call(
        store,
        out_shape=results,
        in_specs=[hbm] * 4,
        out_specs=(hbm,) * 4,
        scratch_shapes=[*(pltpu.VMEM(shape, BF) for shape in shapes), dma((2, 4))],
        compiler_params=pltpu.CompilerParams(vmem_limit_bytes=62 << 20),
        name="store",
    )(*grads)


def solution(mesh):
    split = P("dp", "tensor")
    return jax.shard_map(
        body,
        mesh=mesh,
        in_specs=(split,) * 8 + (P("tensor", "dp"),) * 2 + (P(), P("dp")),
        out_specs=(split,) * 4,
        check_vma=False,
    )
```

```python
import math

import jax
import jax.numpy as jnp
from jax import lax
from jax.experimental import pallas as pl
from jax.experimental.pallas import tpu as pltpu
from jax.sharding import PartitionSpec as P

HD = 128
HEADS = 8
LP = 64
LR = 8
SLOTS = 16
PAIRS = SLOTS // 2
NX, NZ, NC, NY = 4, 8, 2, 8
WROWS = 80
PARTS = 8
PART = 2 * LP // PARTS
SCALE = 1.0 / math.sqrt(HD)
MESH = pl.DeviceIdType.MESH
BF, F32 = jnp.bfloat16, jnp.float32
Z_RANKS = (0, 1, 7, 2, 6, 3, 5, 4)
Z_GROUPS = ((0, 1), (1, 2), (3, 2), (5, 2), (7, 1))
GO_RIGHT = (0, 1, 4)
Y_ORDER = (4, 3, 5, 2, 6, 1, 7)
Y_NEAR = (1, 7, 2, 6, 3, 5, 4)


def dot_nt(a, b):
    return lax.dot_general(a, b, (((1,), (1,)), ((), ())), preferred_element_type=F32)


def dot_nn(a, b):
    return lax.dot_general(a, b, (((1,), (0,)), ((), ())), preferred_element_type=F32)


def dot_tn(a, b):
    return lax.dot_general(a, b, (((0,), (0,)), ((), ())), preferred_element_type=F32)


def rank(k):
    return jnp.where(k == 0, 0, jnp.where(k <= 4, 2 * k - 1, 16 - 2 * k))


def spread_rows(rows):
    lane = lax.broadcasted_iota(jnp.int32, (HEADS, HD), 1) // 16
    head = lax.broadcasted_iota(jnp.int32, (HEADS, HD), 0)
    turned = [rows if k == 0 else pltpu.roll(rows, 16 * k, 1) for k in range(8)]
    out = []
    for pair in range(PAIRS):
        picked = jnp.zeros((HEADS, HD), F32)
        for h in range(HEADS):
            picked = jnp.where((head == h) & (lane == h), turned[(h - pair) % 8], picked)
        out.append(jnp.sum(picked, axis=0, keepdims=True))
    return jnp.concatenate(out, axis=0)


def kernel(
    pk_ref, pv_ref, kw_ref, vw_ref, q_ref, rk_ref, rv_ref, g_ref, lse_ref, delta_ref, prompt_in, len_in,
    dq_out, drk_out, drv_out, input_out,
    dq_ref, drk_ref, drv_ref, out_ref, out_sem, prompt_ref, len_ref, kv, wst, wbuf, q, g, rk, rv, lse, delta, lse_t, delta_t,
    own, sib, table, table_s, snd0, rcv0, snd1, rcv1, snd2, rcv2, rcv3,
    load_sem, table_sem,
    kv_s, kv_r, w0_s, w0_r, wg_s, wg_r,
    rc_s, rc_r, rf_s, rf_r, rn_s, rn_r, rz_s, rz_r, ry_s, ry_r,
):
    me = lax.axis_index("dp")
    t = lax.axis_index("tensor")
    x, z, c = me // 16, (me // 2) % 8, me % 2

    def at(xx, zz, cc):
        return xx * 16 + zz * 2 + cc

    def xp(k):
        return (at((x + k) % NX, z, c), t)

    def zp(k):
        return (at(x, (z + k) % NZ, c), t)

    def yp(k):
        return (me, (t + k) % NY)

    other = (at(x, z, 1 - c), t)

    def remote(src, dst, s, r, dev):
        return pltpu.make_async_remote_copy(src_ref=src, dst_ref=dst, send_sem=s, recv_sem=r, device_id=dev, device_id_type=MESH)

    loads = [
        (pk_ref, kv.at[c, x, 0, 0:LP]),
        (pv_ref, kv.at[c, x, 0, LP : 2 * LP]),
        (kw_ref, wst.at[0:WROWS]),
        (vw_ref, wst.at[WROWS : 2 * WROWS]),
        (q_ref, q),
        (g_ref, g),
        (rk_ref, rk),
        (rv_ref, rv),
        (lse_ref, lse),
        (delta_ref, delta),
        (prompt_in, prompt_ref),
        (len_in, len_ref),
    ]
    loads = [pltpu.make_async_copy(a, b, load_sem.at[i]) for i, (a, b) in enumerate(loads)]
    for copy in loads:
        copy.start()

    w_to = (at((me % 4 + 1) % NX, t, (me // 4) % 2), me // 8)
    w_from = (8 * t + 4 * c + (x + 3) % 4, z)

    barrier = pltpu.get_barrier_semaphore()
    peers = [zp(k) for k in range(1, NZ)] + [xp(k) for k in range(1, NX)] + [yp(k) for k in range(1, NY)]
    peers += [other, w_to, w_from]
    for dev in peers:
        pl.semaphore_signal(barrier, inc=1, device_id=dev, device_id_type=MESH)
    loads[0].wait()
    loads[1].wait()
    loads[2].wait()
    loads[3].wait()
    pl.semaphore_wait(barrier, len(peers))

    sent = []

    def go(copy):
        copy.start()
        sent.append(copy)

    def gather(buf, s, r, ring):
        def copy(n, src, dst, dev):
            return remote(src, dst, s.at[n], r.at[n], dev)

        def over_z(i):
            k = Z_RANKS[i]
            if not ring:
                return copy(i, buf.at[c, x, 0], buf.at[c, x, i], zp(k))
            way = 1 if k <= 4 else -1
            return copy(i, buf.at[c, x, Z_RANKS.index((k - way) % NZ)], buf.at[c, x, i], zp(way % NZ))

        def part(xx, group):
            first, count = Z_GROUPS[group]
            return buf.at[c, xx, pl.ds(first, count)]

        def near(group, way, came=False):
            ref = part((x - way + NX) % NX if came else x, group)
            return copy(8 + 2 * group + (way < 0), ref, ref, xp(way % NX))

        def far(group, came=False):
            way = 1 if group in GO_RIGHT else -1
            ref = part((x - 2 + NX) % NX if came else (x - way + NX) % NX, group)
            return copy(18 + group, ref, ref, xp(way % NX))

        def cross(k, came=False):
            ref = buf.at[1 - c if came else c, (x - k + NX) % NX]
            return copy(23 + k, ref, ref, other)

        def cross_far(half, came=False):
            ref = buf.at[1 - c if came else c, (x - 2 + NX) % NX, pl.ds(5 * half, 5 - 2 * half)]
            return copy(25 if half else 27, ref, ref, other)

        for i in (1, 2) if ring else range(NZ - 1, 0, -1):
            go(over_z(i))
        for way in (1, -1):
            go(near(0, way))
        yield
        for group in range(1, 5):
            first, count = Z_GROUPS[group]
            for i in range(first, first + count):
                over_z(i).wait_recv()
                if ring and i + 2 < NZ:
                    go(over_z(i + 2))
            for way in (1, -1):
                go(near(group, way))
            for way in (1, -1):
                near(group - 1, way, True).wait_recv()
            go(far(group - 1))
            yield
        go(cross(0))
        for way in (1, -1):
            near(4, way, True).wait_recv()
        go(far(4))
        go(cross(1))
        go(cross(3))
        yield
        for half in range(2):
            for group in ((0, 1, 2), (3, 4))[half]:
                far(group, True).wait_recv()
            go(cross_far(half))
        yield
        for k in (0, 1, 3):
            cross(k, True).wait_recv()
        for half in range(2):
            cross_far(half, True).wait_recv()
        yield

    wt_c, wt_z, wt_x = (me // 4) % 2, t, (me % 4 + 1) % NX

    def gather_weights():
        def copy(n, src, dst, dev):
            return remote(src, dst, wg_s.at[n], wg_r.at[n], dev)

        def over_x(k, came=False):
            ref = wbuf.at[c, 0, (x - k + NX) % NX if came else x]
            return copy(k, ref, ref, xp(k))

        def hop(i, way):
            before = Z_RANKS.index((Z_RANKS[i] - way) % NZ)
            if i < NZ - 1:
                return copy(4 + i, wbuf.at[c, before], wbuf.at[c, i], zp(way % NZ))
            part = pl.ds(0 if way == 1 else 2, 2)
            return copy(11 + (way == 1), wbuf.at[c, before, part], wbuf.at[c, i, part], zp(way % NZ))

        def cross(i, came=False):
            ref = wbuf.at[1 - c if came else c, i]
            return copy(13 + i, ref, ref, other)

        go(remote(wst, wbuf.at[wt_c, 0, wt_x], w0_s, w0_r, w_to))
        yield
        remote(wst, wbuf.at[c, 0, x], w0_s, w0_r, w_to).wait_recv()
        for k in (2, 1, 3):
            go(over_x(k))
        yield
        for k in (1, 3, 2):
            over_x(k, True).wait_recv()
        go(hop(1, 1))
        go(hop(2, -1))
        go(cross(0))
        yield
        for i, way in ((1, 1), (2, -1), (3, 1), (4, -1), (5, 1), (6, -1)):
            hop(i, way).wait_recv()
            go(hop(min(i + 2, NZ - 1), way))
            go(cross(i))
            if way == -1:
                yield
        for way in (1, -1):
            hop(NZ - 1, way).wait_recv()
        go(cross(NZ - 1))
        yield
        for i in range(NZ):
            cross(i, True).wait_recv()
        yield

    prompts = gather(kv, kv_s, kv_r, True)
    weights = gather_weights()

    next(prompts)
    next(weights, None)

    next(prompts)
    next(weights, None)
    next(prompts)
    next(prompts)
    next(weights, None)
    next(prompts)
    next(prompts)
    next(prompts)
    next(weights, None)
    for copy in loads[4:]:
        copy.wait()

    lane = lax.broadcasted_iota(jnp.int32, (1, HD), 1)
    rows = []
    for base in (me, at(x, z, 1 - c)):
        found = jnp.full((1, HD), SLOTS, jnp.int32)
        for s in range(SLOTS):
            found = jnp.where(lane == prompt_ref[base * SLOTS + s], s, found)
        rows.append(found)
    table[0:1, :] = rows[0]
    table[1:2, :] = rows[1]
    table_copy = pltpu.make_async_copy(table, table_s, table_sem)
    table_copy.start()
    own[SLOTS] = jnp.zeros((2 * LP, HD), BF)
    sib[SLOTS] = jnp.zeros((2 * LP, HD), BF)

    lse_t[...] = spread_rows(lse[...])
    delta_t[...] = spread_rows(delta[...])

    next(prompts)

    key_row = lax.broadcasted_iota(jnp.int32, (2 * LP + 16, HD), 0)
    column = lax.broadcasted_iota(jnp.int32, (2 * LP + 16, HD), 1)
    col_r, col_t = (column // LR) % 2, column % LR
    in_own = key_row >= 2 * LP
    row_r = jnp.where(in_own, (key_row - 2 * LP) // LR, key_row // LP)
    seen = (row_r == col_r) & (jnp.logical_not(in_own) | ((key_row % LR) <= col_t))
    col_r1, col_t1 = col_r[0:1], col_t[0:1]

    def one_pair(pair):
        base = pl.multiple_of(pair * 16, 16)
        p0, p1 = prompt_ref[me * SLOTS + 2 * pair], prompt_ref[me * SLOTS + 2 * pair + 1]
        l0, l1 = len_ref[2 * pair], len_ref[2 * pair + 1]
        kv0, kv1 = (kv[p % 2, p // 16, rank((z - (p // 2) % 8 + NZ) % NZ)] for p in (p0, p1))
        keys = jnp.concatenate([kv0[:LP], kv1[:LP], rk[pl.ds(base, 16)]], axis=0)
        values = jnp.concatenate([kv0[LP:], kv1[LP:], rv[pl.ds(base, 16)]], axis=0)
        qp = jnp.concatenate([q[pl.ds(base, 16), h * HD : (h + 1) * HD] for h in range(HEADS)], axis=0)
        gp = jnp.concatenate([g[pl.ds(base, 16), h * HD : (h + 1) * HD] for h in range(HEADS)], axis=0)
        live = col_t1 < jnp.where(col_r1 == 0, l0, l1)
        scores = dot_nt(keys, qp) * SCALE
        probs = jnp.exp(scores - lse_t[pl.ds(pair, 1)])
        probs = jnp.where(seen & live, probs, 0.0)
        dprob = dot_nt(values, gp)
        dscore = (probs * (dprob - delta_t[pl.ds(pair, 1)])).astype(BF)
        dv = dot_nn(probs.astype(BF), gp)
        dk = dot_nn(dscore, qp)
        dq = dot_tn(dscore, keys) * SCALE
        for r in range(2):
            own[2 * pair + r, 0:LP] = dk[r * LP : (r + 1) * LP].astype(BF)
            own[2 * pair + r, LP : 2 * LP] = dv[r * LP : (r + 1) * LP].astype(BF)
        drk_ref[pl.ds(base, 16)] = (dk[2 * LP :] * SCALE).astype(BF)
        drv_ref[pl.ds(base, 16)] = dv[2 * LP :].astype(BF)
        for h in range(HEADS):
            dq_ref[pl.ds(base, 16), h * HD : (h + 1) * HD] = dq[h * 16 : (h + 1) * 16].astype(BF)

    def rc(i):
        return remote(own.at[pl.ds(4 * i, 4)], sib.at[pl.ds(4 * i, 4)], rc_s.at[i], rc_r.at[i], other)

    for i in range(4):
        one_pair(2 * i)
        one_pair(2 * i + 1)
        go(rc(i))

    stores = [
        pltpu.make_async_copy(a, b, out_sem.at[i])
        for i, (a, b) in enumerate(
            ((dq_ref, dq_out), (drk_ref, drk_out), (drv_ref, drv_out), (out_ref, input_out))
        )
    ]
    for copy in stores[:3]:
        copy.start()
    table_copy.wait()
    for i in range(4):
        rc(i).wait_recv()

    def both_cores(j, part):
        rows = slice(PART * part, PART * (part + 1))
        return own[table_s[0, j], rows].astype(F32) + sib[table_s[1, j], rows].astype(F32)

    def rf(way, part):
        n = 0 if way == 1 else 1
        return remote(snd0.at[part, n], rcv0.at[part, n], rf_s.at[part, n], rf_r.at[part, n], xp(way % NX))

    def rn(way, part):
        n = 0 if way == 1 else 1
        return remote(snd1.at[part, n], rcv1.at[part, n], rn_s.at[part, n], rn_r.at[part, n], xp(way % NX))

    def rz(i, part):
        return remote(snd2.at[part, i], rcv2.at[part, i], rz_s.at[part, i], rz_r.at[part, i], zp(Z_RANKS[i]))

    def ry(k, part):
        rows = pl.ds(PART * part, PART)
        return remote(rcv3.at[0, rows], rcv3.at[k, rows], ry_s.at[part, k], ry_r.at[part, k], yp(k))

    def ahead(i):
        return (z + Z_RANKS[i]) % NZ

    for part in range(PARTS):
        for way in (1, -1):
            first = 0 if way == 1 else 4
            for i in range(4):
                j = at((x + 2) % NX, ahead(first + i), c)
                snd0[part, first // 4, i] = both_cores(j, part).astype(BF)
            go(rf(way, part))
    next(weights, None)
    for part in range(PARTS):
        for way in (1, -1):
            n = 0 if way == 1 else 1
            for i in [i for i in range(NZ) if i // 4 != n] + [i for i in range(NZ) if i // 4 == n]:
                if i == 4 * n:
                    rf(way, part).wait_recv()
                total = both_cores(at((x + way) % NX, ahead(i), c), part)
                if i // 4 == n:
                    total = total + rcv0[part, n, i - 4 * n].astype(F32)
                snd1[part, n, i] = total.astype(BF)
            go(rn(way, part))
    next(weights, None)

    mine = [None] * PARTS
    for part in range(PARTS):
        for way in (1, -1):
            rn(way, part).wait_recv()
        for i in range(NZ - 1, -1, -1):
            total = both_cores(at(x, ahead(i), c), part)
            for n in range(2):
                total = total + rcv1[part, n, i].astype(F32)
            if i:
                snd2[part, i] = total.astype(BF)
                go(rz(i, part))
            else:
                mine[part] = total
    next(weights, None)
    for part in range(PARTS):
        for i in range(1, NZ):
            rz(i, part).wait_recv()
            mine[part] = mine[part] + rcv2[part, i].astype(F32)
        rcv3[0, PART * part : PART * (part + 1)] = (mine[part] * SCALE if PART * part < LP else mine[part]).astype(BF)
        for k in Y_ORDER:
            go(ry(k, part))
    next(weights, None)

    def project(k):
        head = (t - k + NY) % NY
        place = rank((z - head + NZ) % NZ)
        grads = rcv3[k]
        both = jnp.concatenate([grads[:LP], grads[LP:]], axis=1)
        weights = []
        for cc in range(NC):
            for j in range(4):
                block = wbuf[cc, place, (j + 1) % NX]
                weights.append(jnp.concatenate([block[:WROWS], block[WROWS:]], axis=1))
        return dot_nt(both, jnp.concatenate(weights, axis=0))

    acc = project(0)
    for k in Y_NEAR:
        for part in range(PARTS):
            ry(k, part).wait_recv()
        acc = acc + project(k)
    out_ref[...] = acc.astype(BF)
    stores[3].start()
    for copy in sent:
        copy.wait_send()
    for copy in stores:
        copy.wait()


def store(*refs):
    arrays, outs, tiles, sem = refs[:4], refs[4:8], refs[8:12], refs[12]
    loads = [pltpu.make_async_copy(a, b, sem.at[0, i]) for i, (a, b) in enumerate(zip(arrays, tiles))]
    stores = [pltpu.make_async_copy(a, b, sem.at[1, i]) for i, (a, b) in enumerate(zip(tiles, outs))]
    for copy in loads:
        copy.start()
    for load, copy in zip(loads, stores):
        load.wait()
        copy.start()
    for copy in stores:
        copy.wait()


def body(*args):
    hbm = pl.BlockSpec(memory_space=pl.ANY)
    rows = SLOTS * LR
    dma = pltpu.SemaphoreType.DMA
    shapes = ((rows, HEADS * HD), (rows, HD), (rows, HD), (LP, 8 * WROWS))
    results = tuple(jax.ShapeDtypeStruct(shape, BF) for shape in shapes)
    grads = pl.pallas_call(
        kernel,
        out_shape=results,
        in_specs=[hbm] * 12,
        out_specs=(hbm,) * 4,
        scratch_shapes=[
            *(pltpu.VMEM(shape, BF) for shape in shapes),
            dma((4,)),
            pltpu.SMEM((64 * SLOTS,), jnp.int32),
            pltpu.SMEM((SLOTS,), jnp.int32),
            pltpu.VMEM((NC, NX, NZ, 2 * LP, HD), BF),
            pltpu.VMEM((2 * WROWS, HD), BF),
            pltpu.VMEM((NC, NZ, NX, 2 * WROWS, HD), BF),
            pltpu.VMEM((rows, HEADS * HD), BF),
            pltpu.VMEM((rows, HEADS * HD), BF),
            pltpu.VMEM((rows, HD), BF),
            pltpu.VMEM((rows, HD), BF),
            pltpu.VMEM((HEADS, rows), F32),
            pltpu.VMEM((HEADS, rows), F32),
            pltpu.VMEM((PAIRS, HD), F32),
            pltpu.VMEM((PAIRS, HD), F32),
            pltpu.VMEM((SLOTS + 1, 2 * LP, HD), BF),
            pltpu.VMEM((SLOTS + 1, 2 * LP, HD), BF),
            pltpu.VMEM((8, HD), jnp.int32),
            pltpu.SMEM((8, HD), jnp.int32),
            pltpu.VMEM((PARTS, 2, NZ // 2, PART, HD), BF),
            pltpu.VMEM((PARTS, 2, NZ // 2, PART, HD), BF),
            pltpu.VMEM((PARTS, 2, NZ, PART, HD), BF),
            pltpu.VMEM((PARTS, 2, NZ, PART, HD), BF),
            pltpu.VMEM((PARTS, NZ, PART, HD), BF),
            pltpu.VMEM((PARTS, NZ, PART, HD), BF),
            pltpu.VMEM((NY, 2 * LP, HD), BF),
            dma((12,)),
            dma,
            dma((28,)), dma((28,)), dma, dma, dma((28,)), dma((28,)),
            dma((4,)), dma((4,)), dma((PARTS, 2)), dma((PARTS, 2)), dma((PARTS, 2)), dma((PARTS, 2)),
            dma((PARTS, NZ)), dma((PARTS, NZ)), dma((PARTS, NY)), dma((PARTS, NY)),
        ],
        compiler_params=pltpu.CompilerParams(
            collective_id=0, has_side_effects=True, vmem_limit_bytes=62 << 20
        ),
        name="attention_back",
    )(*args)
    return pl.pallas_call(
        store,
        out_shape=results,
        in_specs=[hbm] * 4,
        out_specs=(hbm,) * 4,
        scratch_shapes=[*(pltpu.VMEM(shape, BF) for shape in shapes), dma((2, 4))],
        compiler_params=pltpu.CompilerParams(vmem_limit_bytes=62 << 20),
        name="store",
    )(*grads)


def solution(mesh):
    split = P("dp", "tensor")
    return jax.shard_map(
        body,
        mesh=mesh,
        in_specs=(split,) * 8 + (P("tensor", "dp"),) * 2 + (P(), P("dp")),
        out_specs=(split,) * 4,
        check_vma=False,
    )
```
